512 devices in a mesh: cube: 4 (over y_hi), row: 16 (over z, core), col: 8 (over y_lo, x).
Axes of the slice: x: 4, y: 8 (y_hi: 4, y_lo: 2; y = y_hi * 2 + y_lo), z: 8, core: 2. Of those that a mesh axis runs over, the one named last changes fastest.
Arguments:
- leaf_front: float32 [16384, 2048], P(('cube', 'row'), 'col'), may hold values from -4 to 4
- leaf_panel: bfloat16 [16384, 1024], P(('cube', 'row'), 'col'), may hold values from -0.625 to 0.625
- leaf_inverse: bfloat16 [4, 1024, 1024], P('cube', 'row', 'col'), as said below
- leaf_fill: int32 [4, 16], replicated, may hold values 0 or 1
- mid_front: float32 [16384, 4096], P(('cube', 'row'), 'col'), may hold values from -4 to 4
- mid_panel: bfloat16 [16384, 1024], P(('cube', 'row'), 'col'), may hold values from -0.625 to 0.625
- mid_inverse: bfloat16 [2, 1024, 1024], P(None, 'row', 'col'), as said below
- mid_fill: int32 [2, 32], replicated, may hold values 0 or 1
- root_front: float32 [16384, 8192], P(('cube', 'row'), 'col'), may hold values from -4 to 4
- root_panel: bfloat16 [16384, 1024], P(('cube', 'row'), 'col'), may hold values from -0.625 to 0.625
- root_inverse: bfloat16 [1024, 1024], P('row', 'col'), as said below
- root_fill: int32 [64], replicated, may hold values 0 or 1
- leaf_map: int32 [4, 16], replicated, may hold values from 0 to 31, as said below
- mid_map: int32 [2, 32], replicated, may hold values from 0 to 63, as said below
Outputs:
- leaf_factor: bfloat16 [16384, 1024], P(('cube', 'row'), 'col')
- mid_factor: bfloat16 [16384, 1024], P(('cube', 'row'), 'col')
- root_factor: bfloat16 [16384, 1024], P(('cube', 'row'), 'col')
- root_update: float32 [16384, 8192], P(('cube', 'row'), 'col')
The draws below stay inside these ranges and needn't reach their ends.
Inputs may be any that keep to these rules, and one draw needn't show every extreme that they name: The blocks of one leaf front go to distinct blocks of its parent; for every i with i % 16 < 8, leaf_map[x, i] % 16 equals i % 16. The blocks of one middle front go to distinct root blocks; for every i with i % 16 < 8, mid_map[x, i] % 16 equals i % 16. `leaf_inverse`: each matrix is lower triangular with its diagonal between 0.5 and 2. `mid_inverse`: lower triangular with its diagonal between 0.5 and 2. `root_inverse`: lower triangular with its diagonal between 0.5 and 2.
All inputs are finite; a program needn't handle non-finite values.
Results may differ from the reference program's by a relative error of at most 0.015.
Values may be sent and summed in bfloat16 or wider, within the bound.
No kernel may reach another device: no remote copies, remote signals or barrier semaphores. Data moves between devices by JAX's collectives and lax.ppermute only.
A program may use at most 64 MiB of HBM per device.

```python
import math
import jax
import jax.numpy as jnp
import numpy as np
from jax import lax

BLK = 256
PANEL = 1024
RB = 1
LEAF_BLOCKS = 16
MID_BLOCKS = 32
ROOT_BLOCKS = 64
LEAF_COLS = 8
MID_COLS = 16
ROOT_COLS = 32
N_ROW = 16
N_COL = 8


def lower_inverse(diagonal, lower):
    shape = diagonal.shape
    rows = lax.broadcasted_iota(jnp.int32, shape, len(shape) - 2)
    columns = lax.broadcasted_iota(jnp.int32, shape, len(shape) - 1)
    scale = 0.5 / math.sqrt(PANEL)
    result = jnp.where(rows == columns, diagonal, jnp.where(columns < rows, scale * lower, 0.0))
    return result.astype(jnp.float32).astype(jnp.bfloat16)


def block_map(key, fronts, child_blocks, parent_blocks, stride, window):
    child_slots = child_blocks // stride
    parent_slots = parent_blocks // stride
    raw_scores = jax.random.randint(key, (fronts, parent_blocks), 0, 1 << 20)
    position = lax.broadcasted_iota(jnp.int32, (fronts, parent_blocks), 1)
    front_index = lax.broadcasted_iota(jnp.int32, (fronts, parent_blocks), 0)
    scores = raw_scores * parent_blocks + position
    scores = jnp.where((front_index == 0) & (position == 0), -1, scores)
    scores = jnp.where((front_index == 0) & (position == parent_blocks - 1), -1, scores)
    ceiling = (1 << 20) * parent_blocks + parent_blocks
    far_residue = (window + stride // 2) % stride
    special = (front_index == 0) & (position == stride * (parent_slots - 1) + far_residue)
    slot_scores = jnp.where(special, ceiling, scores)
    slot_order = jnp.argsort(slot_scores.reshape(fronts, parent_slots, stride), axis=1).astype(jnp.int32)
    slot_rank = jnp.argsort(slot_order, axis=1).astype(jnp.int32)
    residue = lax.broadcasted_iota(jnp.int32, (fronts, parent_slots, stride), 2)
    chosen = ((slot_rank < child_slots) & (residue < window)).reshape(fronts, parent_blocks)
    spare_scores = jnp.where(chosen, ceiling + 1, jnp.where(special, -3, scores))
    spare_blocks = jnp.argsort(spare_scores, axis=1).astype(jnp.int32)
    spare_blocks = spare_blocks[:, :child_slots * (stride - window)]
    window_targets = stride * slot_order[:, :child_slots, :window] + jnp.arange(window, dtype=jnp.int32)[None, None, :]
    window_index = np.array([stride * slot_index + residue_index for slot_index in range(child_slots) for residue_index in range(window)], dtype=np.int32)
    other_index = np.array([stride * slot_index + residue_index for slot_index in range(child_slots) for residue_index in range(window, stride)], dtype=np.int32)
    result = jnp.zeros((fronts, child_blocks), jnp.int32)
    result = result.at[:, window_index].set(window_targets.reshape(fronts, -1))
    result = result.at[:, other_index].set(spare_blocks)
    return result.astype(jnp.int32)


def draw_leaf_inverse(key, part):
    key = jax.random.fold_in(key, 5)
    first, second = jax.random.split(key)
    shape = (4, PANEL, PANEL)
    diagonal = jnp.exp(jax.random.uniform(first, shape, jnp.float32, -0.69, 0.69))
    lower = jax.random.normal(second, shape, jnp.float32)
    return lower_inverse(diagonal, lower)


def draw_mid_inverse(key, part):
    key = jax.random.fold_in(key, 6)
    first, second = jax.random.split(key)
    shape = (2, PANEL, PANEL)
    diagonal = jnp.exp(jax.random.uniform(first, shape, jnp.float32, -0.69, 0.69))
    lower = jax.random.normal(second, shape, jnp.float32)
    return lower_inverse(diagonal, lower)


def draw_root_inverse(key, part):
    key = jax.random.fold_in(key, 7)
    first, second = jax.random.split(key)
    shape = (PANEL, PANEL)
    diagonal = jnp.exp(jax.random.uniform(first, shape, jnp.float32, -0.69, 0.69))
    lower = jax.random.normal(second, shape, jnp.float32)
    return lower_inverse(diagonal, lower)


def draw_leaf_map(key, part):
    key = jax.random.fold_in(key, 21)
    return block_map(key, 4, LEAF_BLOCKS, MID_BLOCKS, LEAF_BLOCKS // RB, LEAF_COLS // RB)


def draw_mid_map(key, part):
    key = jax.random.fold_in(key, 22)
    return block_map(key, 2, MID_BLOCKS, ROOT_BLOCKS, LEAF_BLOCKS // RB, LEAF_COLS // RB)


def touch_ends(drawn, rng, least, largest):
    dims = drawn.shape
    index_at = [jax.random.randint(jax.random.fold_in(rng, axis), (), 0, dims[axis]) for axis in range(len(dims))]
    drawn = drawn.at[tuple(index_at)].set(least)
    longest = dims.index(max(dims))
    index_at[longest] = (index_at[longest] + 1) % dims[longest]
    return drawn.at[tuple(index_at)].set(largest)


def shard_levels(rng, extent, pieces, least, top_value):
    level = 1.0
    for axis_at, blocks in pieces:
        heights = jax.random.uniform(jax.random.fold_in(jax.random.fold_in(rng, 6), axis_at), (blocks,), jnp.float32, least / len(pieces), top_value / len(pieces))
        level = level * jnp.repeat(jnp.exp(heights), extent[axis_at] // blocks).reshape((-1,) + (1,) * (len(extent) - 1 - axis_at))
    return level


def normal_values(stream_key, shape, spread, most, cuts=(), held_as=jnp.bfloat16):
    gain = shard_levels(stream_key, shape, cuts, -0.22, 0.18) if cuts else 1.0
    values = jax.random.normal(stream_key, shape, jnp.float32) * spread * gain
    return jnp.minimum(jnp.maximum(values, -most), most).astype(held_as)


def setup_inputs(seed: int = 0) -> dict:
    seeds = jax.random.split(jax.random.key(seed), 15)
    return {
        "leaf_front": normal_values(seeds[0], (4 * LEAF_BLOCKS * BLK, LEAF_COLS * BLK), 0.3, 4.0, ((0, 64), (1, 8)), jnp.float32),
        "leaf_panel": normal_values(seeds[1], (4 * LEAF_BLOCKS * BLK, PANEL), 0.04, 0.625, ((0, 64), (1, 8))),
        "leaf_inverse": draw_leaf_inverse(jax.random.fold_in(seeds[14], 71), 0),
        "leaf_fill": touch_ends((jax.random.randint(seeds[3], (4, LEAF_BLOCKS), 0, 4) < 3).astype(jnp.int32), jax.random.fold_in(seeds[3], 1), 0, 1),
        "mid_front": normal_values(seeds[4], (2 * MID_BLOCKS * BLK, MID_COLS * BLK), 0.3, 4.0, ((0, 64), (1, 8)), jnp.float32),
        "mid_panel": normal_values(seeds[5], (2 * MID_BLOCKS * BLK, PANEL), 0.04, 0.625, ((0, 64), (1, 8))),
        "mid_inverse": draw_mid_inverse(jax.random.fold_in(seeds[14], 71), 0),
        "mid_fill": touch_ends((jax.random.randint(seeds[7], (2, MID_BLOCKS), 0, 4) < 3).astype(jnp.int32), jax.random.fold_in(seeds[7], 1), 0, 1),
        "root_front": normal_values(seeds[8], (ROOT_BLOCKS * BLK, ROOT_COLS * BLK), 0.3, 4.0, ((0, 64), (1, 8)), jnp.float32),
        "root_panel": normal_values(seeds[9], (ROOT_BLOCKS * BLK, PANEL), 0.04, 0.625, ((0, 64), (1, 8))),
        "root_inverse": draw_root_inverse(jax.random.fold_in(seeds[14], 71), 0),
        "root_fill": touch_ends((jax.random.randint(seeds[11], (ROOT_BLOCKS,), 0, 4) < 3).astype(jnp.int32), jax.random.fold_in(seeds[11], 1), 0, 1),
        "leaf_map": draw_leaf_map(jax.random.fold_in(seeds[14], 71), 0),
        "mid_map": draw_mid_map(jax.random.fold_in(seeds[14], 71), 0),
    }


def rows_natural(stored, owners):
    width = stored.shape[1]
    return stored.reshape(owners, RB, BLK, width).transpose(1, 0, 2, 3).reshape(owners * RB * BLK, width)


def rows_stored(natural, owners):
    width = natural.shape[1]
    return natural.reshape(RB, owners, BLK, width).transpose(1, 0, 2, 3).reshape(owners * RB * BLK, width)


def cols_natural(stored, slots):
    height = stored.shape[0]
    return stored.reshape(height, N_COL, slots, BLK).transpose(0, 2, 1, 3).reshape(height, slots * N_COL * BLK)


def cols_stored(natural, slots):
    height = natural.shape[0]
    return natural.reshape(height, slots, N_COL, BLK).transpose(0, 2, 1, 3).reshape(height, N_COL * slots * BLK)


def window_blocks(slots):
    return np.array([N_ROW * slot_index + column_index for slot_index in range(slots) for column_index in range(N_COL)], dtype=np.int32)


def factor_of(panel, inverse, fill):
    width = PANEL // N_COL
    total = jnp.zeros((panel.shape[0], PANEL), jnp.float32)
    for column_index in range(N_COL):
        left = panel[:, column_index * width:(column_index + 1) * width].astype(jnp.float32)
        right = inverse[:, column_index * width:(column_index + 1) * width].astype(jnp.float32)
        partial_value = jnp.dot(left, right.T, preferred_element_type=jnp.float32)
        total = total + lax.optimization_barrier(partial_value.astype(jnp.bfloat16)).astype(jnp.float32)
    weights = jnp.repeat(fill.astype(jnp.float32), BLK)
    return (total * weights[:, None]).astype(jnp.bfloat16)


def schur_of(factor, slots):
    chosen = factor.reshape(-1, BLK, PANEL)[window_blocks(slots)].reshape(-1, PANEL)
    return jnp.dot(factor.astype(jnp.float32), chosen.astype(jnp.float32).T, preferred_element_type=jnp.float32)


def assemble(updates, mappings, parent_blocks):
    parent_slots = parent_blocks // N_ROW
    total = jnp.zeros((parent_blocks, parent_slots * N_COL, BLK, BLK), jnp.float32)
    for update, mapping in zip(updates, mappings):
        child_blocks = mapping.shape[0]
        child_slots = child_blocks // N_ROW
        tiles = update.astype(jnp.float32).reshape(child_blocks, BLK, child_slots * N_COL, BLK).transpose(0, 2, 1, 3)
        targets = mapping[window_blocks(child_slots)]
        columns = (targets // N_ROW) * N_COL + targets % N_ROW
        total = total.at[mapping[:, None], columns[None, :]].add(tiles)
    return total.transpose(0, 2, 1, 3).reshape(parent_blocks * BLK, parent_slots * N_COL * BLK)


def reference(leaf_front, leaf_panel, leaf_inverse, leaf_fill, mid_front, mid_panel, mid_inverse, mid_fill, root_front, root_panel, root_inverse, root_fill, leaf_map, mid_map):
    leaf_height = RB * N_ROW * BLK
    leaf_factors = []
    leaf_updates = []
    for front in range(4):
        panel = rows_natural(leaf_panel[front * leaf_height:(front + 1) * leaf_height], N_ROW)
        factor = factor_of(panel, leaf_inverse[front], leaf_fill[front])
        matrix = cols_natural(rows_natural(leaf_front[front * leaf_height:(front + 1) * leaf_height], N_ROW), RB)
        leaf_updates.append((matrix - schur_of(factor, RB)).astype(jnp.bfloat16))
        leaf_factors.append(rows_stored(factor, N_ROW))
    mid_height = 2 * leaf_height
    mid_factors = []
    mid_updates = []
    for front in range(2):
        panel = rows_natural(mid_panel[front * mid_height:(front + 1) * mid_height], 2 * N_ROW)
        factor = factor_of(panel, mid_inverse[front], mid_fill[front])
        matrix = cols_natural(rows_natural(mid_front[front * mid_height:(front + 1) * mid_height], 2 * N_ROW), 2 * RB)
        assembled = assemble(leaf_updates[2 * front:2 * front + 2], [leaf_map[2 * front], leaf_map[2 * front + 1]], 2 * RB * N_ROW)
        mid_updates.append((matrix + assembled - schur_of(factor, 2 * RB)).astype(jnp.bfloat16))
        mid_factors.append(rows_stored(factor, 2 * N_ROW))
    panel = rows_natural(root_panel, 4 * N_ROW)
    factor = factor_of(panel, root_inverse, root_fill)
    matrix = cols_natural(rows_natural(root_front, 4 * N_ROW), 4 * RB)
    assembled = assemble(mid_updates, [mid_map[0], mid_map[1]], 4 * RB * N_ROW)
    updated = matrix + assembled - schur_of(factor, 4 * RB)
    root_update = cols_stored(rows_stored(updated, 4 * N_ROW), 4 * RB)
    return (jnp.concatenate(leaf_factors, 0), jnp.concatenate(mid_factors, 0), rows_stored(factor, 4 * N_ROW), root_update)
```

```python
import jax
import jax.numpy as jnp
from jax import lax
from jax.experimental import pallas as pl
from jax.experimental.pallas import tpu as pltpu
from jax.sharding import Mesh, PartitionSpec as P

CUBE = ("pair", "half")
ROW = ("z", "core")
COL = ("ylo", "x")
VMEM = pl.BlockSpec(memory_space=pltpu.VMEM)
SMEM = pl.BlockSpec(memory_space=pltpu.SMEM)
BF = jnp.bfloat16
F32 = jnp.float32


def params():
    return pltpu.CompilerParams(vmem_limit_bytes=40 * 1024 * 1024)


def shape(dims, dtype=BF):
    return jax.ShapeDtypeStruct(dims, dtype)


def dot_t(left, right):
    return lax.dot_general(left, right, (((1,), (1,)), ((), ())), preferred_element_type=F32)


def weights_kernel(where, leaf, mid, root, out):
    pair = where[0] // 2
    for to in range(8):
        out[to, 0] = leaf[0]
        out[to, 1] = mid[pair]
        out[to, 2] = root[...]


def partial_kernel(where, leaf, mid, root, own, other, out):
    first = where[1] % 2 == 0
    for front, panel in enumerate((leaf, mid, root)):
        for group in range(0, 8, 2):
            rows = []
            for at in (group, group + 1):
                mine, theirs = own[at, front], other[at, front]
                rows.append(jnp.where(first, mine, theirs))
                rows.append(jnp.where(first, theirs, mine))
            product = dot_t(panel[...], jnp.concatenate(rows, 0)).astype(BF)
            out[group, front] = product[:, :128]
            out[group + 1, front] = product[:, 128:]


def factor_kernel(where, leaf_fill, mid_fill, root_fill, parts, leaf, mid, root, spread, low, high):
    cube, row = where[0], where[1]
    fills = (
        leaf_fill[cube, row],
        mid_fill[cube // 2, 16 * (cube % 2) + row],
        root_fill[16 * cube + row],
    )
    for front, target in enumerate((leaf, mid, root)):
        total = parts[0, front].astype(F32)
        for at in range(1, 8):
            total = total + parts[at, front].astype(F32)
        value = (total * fills[front].astype(F32)).astype(BF)
        target[...] = value
        for to in range(8):
            spread[to, front] = value
        low[front] = value[:128]
        high[front] = value[128:]


def update_kernel(where, factors, own, other, leaf_front, mid_front, out, rows, columns):
    first = where[1] % 2 == 0
    for front in range(2):
        for at in range(8):
            rows[front, :, 128 * at : 128 * at + 128] = factors[at, front]
    for kind in range(3):
        for at in range(8):
            half, group = at // 4, 2 * (at % 4)
            mine, theirs = own[at, kind], other[at, kind]
            span = slice(128 * half, 128 * half + 128)
            columns[kind, span, 128 * group : 128 * group + 128] = jnp.where(first, mine, theirs)
            columns[kind, span, 128 * group + 128 : 128 * group + 256] = jnp.where(
                first, theirs, mine
            )
    for kind in range(3):
        product = dot_t(rows[min(kind, 1)], columns[kind])
        if kind == 0:
            matrix = leaf_front[...]
        else:
            matrix = mid_front[:, 256 * (kind - 1) : 256 * kind]
        value = matrix - product
        for side in range(2):
            piece = value[:, 128 * side : 128 * side + 128].reshape(32, 8, 128)
            out[:, side, kind] = piece.astype(BF)


def place_kernel(where, leaf_map, mid_map, pieces, out, total):
    column = where[2]
    total[...] = jnp.zeros_like(total)
    for front in range(4):
        pair = front // 2
        slot = mid_map[pair, leaf_map[front, column]] // 16
        for block in range(16):
            target = mid_map[pair, leaf_map[front, block]]
            total[4 * target + slot] += pieces[16 * front + block, 0].astype(F32)
    for pair in range(2):
        slots = [mid_map[pair, 16 * at + column] // 16 for at in range(2)]
        for block in range(32):
            target = mid_map[pair, block]
            for at in range(2):
                total[4 * target + slots[at]] += pieces[32 * pair + block, 1 + at].astype(F32)
    out[...] = total[...].reshape(64, 4, 8, 128).astype(BF)


def root_kernel(factors, blocks, arrived, front, out, rows, columns):
    @pl.when(pl.program_id(0) == 0)
    def _():
        for at in range(8):
            rows[:, 128 * at : 128 * at + 128] = factors[at, 0]

    for half in range(2):
        for at in range(8):
            columns[128 * half : 128 * half + 128, 128 * at : 128 * at + 128] = blocks[
                8 * half + at
            ]
    value = front[...] - dot_t(rows[...], columns[...])
    for side in range(2):
        added = arrived[:, side, 0].astype(F32).reshape(256, 128)
        span = slice(128 * side, 128 * side + 128)
        out[:, span] = value[:, span] + added


def swap(value, axis):
    return lax.ppermute(value, axis, [(0, 1), (1, 0)])


def transpose(low, high):
    to_low = [(8 * r + c, 8 * c + r) for r in range(8) for c in range(8)]
    to_high = [(8 * r + c, 8 * (c + 8) + r) for r in range(8) for c in range(8)]
    return lax.ppermute(low, ROW + COL, to_low), lax.ppermute(high, ROW + COL, to_high)


def local(
    leaf_front,
    leaf_panel,
    leaf_inverse,
    leaf_fill,
    mid_front,
    mid_panel,
    mid_inverse,
    mid_fill,
    root_front,
    root_panel,
    root_inverse,
    root_fill,
    leaf_map,
    mid_map,
):
    row = lax.axis_index(ROW)
    where = jnp.stack([lax.axis_index(CUBE), row, lax.axis_index(COL)]).astype(jnp.int32)

    weights = pl.pallas_call(
        weights_kernel,
        out_shape=shape((8, 3, 64, 128)),
        in_specs=[SMEM, VMEM, VMEM, VMEM],
        out_specs=VMEM,
        compiler_params=params(),
    )(where, leaf_inverse, mid_inverse, root_inverse)
    own = lax.all_to_all(weights, "z", 0, 0, tiled=True)
    other = swap(own, "core")
    partials = pl.pallas_call(
        partial_kernel,
        out_shape=shape((8, 3, 256, 128)),
        in_specs=[SMEM] + [VMEM] * 5,
        out_specs=VMEM,
        compiler_params=params(),
    )(where, leaf_panel, mid_panel, root_panel, own, other)
    partials = lax.all_to_all(partials, COL, 0, 0, tiled=True)
    piece = shape((256, 128))
    leaf_factor, mid_factor, root_factor, spread, low, high = pl.pallas_call(
        factor_kernel,
        out_shape=(piece, piece, piece, shape((8, 3, 256, 128)), shape((3, 128, 128)), shape((3, 128, 128))),
        in_specs=[SMEM] * 4 + [VMEM],
        out_specs=(VMEM,) * 6,
        compiler_params=params(),
    )(where, leaf_fill, mid_fill, root_fill, partials)

    low, high = transpose(low, high)
    factors = lax.all_to_all(spread, COL, 0, 0, tiled=True)
    turned = jnp.where(row < 8, low, high)
    root_blocks = lax.all_gather(turned[2], CUBE + ROW, axis=0, tiled=False)
    half = lax.axis_index("half")
    partner = swap(turned[1], "half")
    first = jnp.where(half == 0, turned[1], partner)
    second = jnp.where(half == 0, partner, turned[1])
    sent = jnp.stack([turned[0], first, second])
    own = lax.all_to_all(jnp.broadcast_to(sent[None], (8, 3, 128, 128)), "z", 0, 0, tiled=True)
    other = swap(own, "core")
    updates = pl.pallas_call(
        update_kernel,
        out_shape=shape((32, 2, 3, 8, 128)),
        in_specs=[SMEM] + [VMEM] * 5,
        out_specs=VMEM,
        scratch_shapes=[pltpu.VMEM((2, 256, 1024), BF), pltpu.VMEM((3, 256, 1024), BF)],
        compiler_params=params(),
    )(where, factors, own, other, leaf_front, mid_front)
    pieces = lax.all_to_all(updates.reshape(64, 3, 8, 128), CUBE + ROW, 0, 0, tiled=True)
    placed = pl.pallas_call(
        place_kernel,
        out_shape=shape((64, 4, 8, 128)),
        in_specs=[SMEM] * 3 + [VMEM],
        out_specs=VMEM,
        scratch_shapes=[pltpu.VMEM((256, 8, 128), F32)],
        compiler_params=params(),
    )(where, leaf_map, mid_map, pieces)
    arrived = lax.all_to_all(placed, CUBE + ROW, 0, 0, tiled=True)
    root_update = pl.pallas_call(
        root_kernel,
        grid=(4,),
        out_shape=shape((256, 1024), F32),
        in_specs=[
            pl.BlockSpec((8, 1, 256, 128), lambda s: (0, 2, 0, 0)),
            pl.BlockSpec((16, 128, 128), lambda s: (s, 0, 0)),
            pl.BlockSpec((32, 2, 1, 8, 128), lambda s: (0, 0, s, 0, 0)),
            pl.BlockSpec((256, 256), lambda s: (0, s)),
        ],
        out_specs=pl.BlockSpec((256, 256), lambda s: (0, s)),
        scratch_shapes=[pltpu.VMEM((256, 1024), BF), pltpu.VMEM((256, 1024), BF)],
        compiler_params=params(),
    )(factors, root_blocks, arrived.reshape(32, 2, 4, 8, 128), root_front)
    return leaf_factor, mid_factor, root_factor, root_update


def solution(mesh):
    fine = Mesh(
        mesh.devices.reshape(2, 2, 8, 2, 2, 4), ("pair", "half", "z", "core", "ylo", "x")
    )
    block = P(CUBE + ROW, COL)
    in_specs = (
        block,
        block,
        P(CUBE, ROW, COL),
        P(),
        block,
        block,
        P(None, ROW, COL),
        P(),
        block,
        block,
        P(ROW, COL),
        P(),
        P(),
        P(),
    )
    return jax.shard_map(
        local, mesh=fine, in_specs=in_specs, out_specs=(block,) * 4, check_vma=False
    )
```

```python
import jax
import jax.numpy as jnp
from jax import lax
from jax.experimental import pallas as pl
from jax.experimental.pallas import tpu as pltpu
from jax.sharding import Mesh, PartitionSpec as P

CUBE = ("pair", "half")
ROW = ("z", "core")
COL = ("ylo", "x")
VMEM = pl.BlockSpec(memory_space=pltpu.VMEM)
SMEM = pl.BlockSpec(memory_space=pltpu.SMEM)
BF = jnp.bfloat16
F32 = jnp.float32


ANY = pl.BlockSpec(memory_space=pl.ANY)


def params(mebibytes=40):
    return pltpu.CompilerParams(vmem_limit_bytes=mebibytes * 1024 * 1024)


def shape(dims, dtype=BF):
    return jax.ShapeDtypeStruct(dims, dtype)


def dot_t(left, right):
    return lax.dot_general(left, right, (((1,), (1,)), ((), ())), preferred_element_type=F32)


def weights_kernel(where, leaf, mid, root, leaf_panel, mid_panel, root_panel, out, panels):
    pair = where[0] // 2
    panels[0] = leaf_panel[...]
    panels[1] = mid_panel[...]
    panels[2] = root_panel[...]
    for to in range(8):
        out[to, 0] = leaf[0]
        out[to, 1] = mid[pair]
        out[to, 2] = root[...]


def partial_kernel(where, panels, own, other, out):
    first = where[1] % 2 == 0
    for front in range(3):
        for group in range(0, 8, 2):
            rows = []
            for at in (group, group + 1):
                mine, theirs = own[at, front], other[at, front]
                rows.append(jnp.where(first, mine, theirs))
                rows.append(jnp.where(first, theirs, mine))
            product = dot_t(panels[front], jnp.concatenate(rows, 0)).astype(BF)
            out[group, front] = product[:, :128]
            out[group + 1, front] = product[:, 128:]


def factor_kernel(where, leaf_fill, mid_fill, root_fill, parts, leaf, mid, root, spread, low, high, low_two, high_two):
    cube, row = where[0], where[1]
    fills = (
        leaf_fill[cube, row],
        mid_fill[cube // 2, 16 * (cube % 2) + row],
        root_fill[16 * cube + row],
    )
    for front, target in enumerate((leaf, mid, root)):
        total = parts[0, front].astype(F32)
        for at in range(1, 8):
            total = total + parts[at, front].astype(F32)
        value = (total * fills[front].astype(F32)).astype(BF)
        target[...] = value
        for to in range(8):
            spread[to, front] = value
        low[front] = value[:128]
        high[front] = value[128:]
        if front > 0:
            low_two[front - 1] = value[:128]
            high_two[front - 1] = value[128:]


def turn_kernel(where, low, high, low_two, high_two, after, sent, root):
    cube, row = where[0], where[1]
    own = [jnp.where(row < 8, low[front], high[front]) for front in range(3)]
    partner = [jnp.where(row < 8, low_two[front], high_two[front]) for front in range(2)]
    even = cube % 2 == 0
    first, second = jnp.where(even, own[1], partner[0]), jnp.where(even, partner[0], own[1])
    for to in range(8):
        sent[to, 0] = own[0]
        sent[to, 1] = first
        sent[to, 2] = second
    root[0] = jnp.where(even, own[2], partner[1])
    root[1] = jnp.where(even, partner[1], own[2])


def update_kernel(where, factors, own, other, leaf_front, mid_front, out, rows, columns):
    first = where[1] % 2 == 0
    for front in range(2):
        for at in range(8):
            rows[front, :, 128 * at : 128 * at + 128] = factors[at, front]
    for kind in range(3):
        for at in range(8):
            half, group = at // 4, 2 * (at % 4)
            mine, theirs = own[at, kind], other[at, kind]
            span = slice(128 * half, 128 * half + 128)
            columns[kind, span, 128 * group : 128 * group + 128] = jnp.where(first, mine, theirs)
            columns[kind, span, 128 * group + 128 : 128 * group + 256] = jnp.where(
                first, theirs, mine
            )
    for kind in range(3):
        product = dot_t(rows[min(kind, 1)], columns[kind])
        if kind == 0:
            matrix = leaf_front[...]
        else:
            matrix = mid_front[:, 256 * (kind - 1) : 256 * kind]
        value = matrix - product
        for side in range(2):
            piece = value[:, 128 * side : 128 * side + 128].reshape(32, 8, 128)
            out[:, side, kind] = piece.astype(BF)


def place_kernel(where, leaf_map, mid_map, pieces, out, total):
    column = where[2]
    total[...] = jnp.zeros_like(total)
    for front in range(4):
        pair = front // 2
        slot = mid_map[pair, leaf_map[front, column]] // 16
        for block in range(16):
            target = mid_map[pair, leaf_map[front, block]]
            total[4 * target + slot] += pieces[16 * front + block, 0].astype(F32)
    for pair in range(2):
        slots = [mid_map[pair, 16 * at + column] // 16 for at in range(2)]
        for block in range(32):
            target = mid_map[pair, block]
            for at in range(2):
                total[4 * target + slots[at]] += pieces[32 * pair + block, 1 + at].astype(F32)
    out[...] = total[...].reshape(64, 4, 8, 128).astype(BF)


def root_kernel(factors, blocks, front, out, rows, columns):
    @pl.when(pl.program_id(0) == 0)
    def _():
        for at in range(8):
            rows[:, 128 * at : 128 * at + 128] = factors[at, 0]

    for half in range(2):
        for at in range(8):
            columns[128 * half : 128 * half + 128, 128 * at : 128 * at + 128] = blocks[
                8 * half + at, 0
            ]
    out[...] = front[...] - dot_t(rows[...], columns[...])


def add_kernel(base, arrived, out):
    for side in range(2):
        added = arrived[:, side, 0].astype(F32).reshape(256, 128)
        span = slice(128 * side, 128 * side + 128)
        out[:, span] = base[:, span] + added


def swap(value, axis):
    return lax.ppermute(value, axis, [(0, 1), (1, 0)])


def transpose(low, high, low_two, high_two):
    low_pairs, high_pairs, low_cross, high_cross = [], [], [], []
    for r in range(8):
        for c in range(8):
            low_pairs.append((8 * r + c, 8 * c + r))
            high_pairs.append((8 * r + c, 8 * (c + 8) + r))
            for half in range(2):
                source = 128 * half + 8 * r + c
                low_cross.append((source, 128 * (1 - half) + 8 * c + r))
                high_cross.append((source, 128 * (1 - half) + 8 * (c + 8) + r))
    plane = ROW + COL
    return (
        lax.ppermute(low, plane, low_pairs),
        lax.ppermute(high, plane, high_pairs),
        lax.ppermute(low_two, ("half",) + plane, low_cross),
        lax.ppermute(high_two, ("half",) + plane, high_cross),
    )


def local(
    leaf_front,
    leaf_panel,
    leaf_inverse,
    leaf_fill,
    mid_front,
    mid_panel,
    mid_inverse,
    mid_fill,
    root_front,
    root_panel,
    root_inverse,
    root_fill,
    leaf_map,
    mid_map,
):
    row = lax.axis_index(ROW)
    where = jnp.stack([lax.axis_index(CUBE), row, lax.axis_index(COL)]).astype(jnp.int32)

    weights, panels = pl.pallas_call(
        weights_kernel,
        out_shape=(shape((8, 3, 64, 128)), shape((3, 256, 128))),
        in_specs=[SMEM] + [VMEM] * 6,
        out_specs=(VMEM, VMEM),
        compiler_params=params(60),
    )(where, leaf_inverse, mid_inverse, root_inverse, leaf_panel, mid_panel, root_panel)
    own = lax.all_to_all(weights, "z", 0, 0, tiled=True)
    other = swap(own, "core")
    partials = pl.pallas_call(
        partial_kernel,
        out_shape=shape((8, 3, 256, 128)),
        in_specs=[SMEM] + [VMEM] * 3,
        out_specs=VMEM,
        compiler_params=params(),
    )(where, panels, own, other)
    partials = lax.all_to_all(partials, COL, 0, 0, tiled=True)
    piece, three, two = shape((256, 128)), shape((3, 128, 128)), shape((2, 128, 128))
    leaf_factor, mid_factor, root_factor, spread, *pieces = pl.pallas_call(
        factor_kernel,
        out_shape=(piece, piece, piece, shape((8, 3, 256, 128)), three, three, two, two),
        in_specs=[SMEM] * 4 + [VMEM],
        out_specs=(VMEM,) * 8,
        compiler_params=params(),
    )(where, leaf_fill, mid_fill, root_fill, partials)

    pieces = transpose(*pieces)
    factors = lax.all_to_all(spread, COL, 0, 0, tiled=True)
    sent, root_pair = pl.pallas_call(
        turn_kernel,
        out_shape=(shape((8, 3, 128, 128)), two),
        in_specs=[SMEM] + [VMEM] * 4 + [ANY],
        out_specs=(VMEM, VMEM),
        compiler_params=params(),
    )(where, *pieces, factors)
    root_other = swap(root_pair, "pair")
    own = lax.all_to_all(sent, "z", 0, 0, tiled=True)
    pair = lax.axis_index("pair")
    root_four = jnp.where(
        pair == 0,
        jnp.concatenate([root_pair, root_other]),
        jnp.concatenate([root_other, root_pair]),
    )
    root_blocks = lax.all_gather(root_four, ROW, axis=0, tiled=False)
    other = swap(own, "core")
    updates = pl.pallas_call(
        update_kernel,
        out_shape=shape((32, 2, 3, 8, 128)),
        in_specs=[SMEM] + [VMEM] * 5,
        out_specs=VMEM,
        scratch_shapes=[pltpu.VMEM((2, 256, 1024), BF), pltpu.VMEM((3, 256, 1024), BF)],
        compiler_params=params(),
    )(where, factors, own, other, leaf_front, mid_front)
    pieces = lax.all_to_all(updates.reshape(64, 3, 8, 128), CUBE + ROW, 0, 0, tiled=True)
    placed = pl.pallas_call(
        place_kernel,
        out_shape=shape((64, 4, 8, 128)),
        in_specs=[SMEM] * 3 + [VMEM],
        out_specs=VMEM,
        scratch_shapes=[pltpu.VMEM((256, 8, 128), F32)],
        compiler_params=params(),
    )(where, leaf_map, mid_map, pieces)
    arrived = lax.all_to_all(placed, CUBE + ROW, 0, 0, tiled=True)
    spot = pl.BlockSpec((256, 256), lambda s: (0, s))
    base = pl.pallas_call(
        root_kernel,
        grid=(4,),
        out_shape=shape((256, 1024), F32),
        in_specs=[
            pl.BlockSpec((8, 1, 256, 128), lambda s: (0, 2, 0, 0)),
            pl.BlockSpec((16, 1, 128, 128), lambda s: (0, s, 0, 0)),
            spot,
        ],
        out_specs=spot,
        scratch_shapes=[pltpu.VMEM((256, 1024), BF), pltpu.VMEM((256, 1024), BF)],
        compiler_params=params(60),
        cost_estimate=pl.CostEstimate(flops=2**29, bytes_accessed=2**22, transcendentals=0),
    )(factors, root_blocks, root_front)
    root_update = pl.pallas_call(
        add_kernel,
        grid=(4,),
        out_shape=shape((256, 1024), F32),
        in_specs=[spot, pl.BlockSpec((32, 2, 1, 8, 128), lambda s: (0, 0, s, 0, 0))],
        out_specs=spot,
        compiler_params=params(),
    )(base, arrived.reshape(32, 2, 4, 8, 128))
    return leaf_factor, mid_factor, root_factor, root_update


def solution(mesh):
    fine = Mesh(
        mesh.devices.reshape(2, 2, 8, 2, 2, 4), ("pair", "half", "z", "core", "ylo", "x")
    )
    block = P(CUBE + ROW, COL)
    in_specs = (
        block,
        block,
        P(CUBE, ROW, COL),
        P(),
        block,
        block,
        P(None, ROW, COL),
        P(),
        block,
        block,
        P(ROW, COL),
        P(),
        P(),
        P(),
    )
    return jax.shard_map(
        local, mesh=fine, in_specs=in_specs, out_specs=(block,) * 4, check_vma=False
    )
```

```python
import jax
import jax.numpy as jnp
from jax import lax
from jax.experimental import pallas as pl
from jax.experimental.pallas import tpu as pltpu
from jax.sharding import Mesh, PartitionSpec as P

CUBE = ("pair", "half")
ROW = ("z", "core")
COL = ("ylo", "x")
VMEM = pl.BlockSpec(memory_space=pltpu.VMEM)
SMEM = pl.BlockSpec(memory_space=pltpu.SMEM)
BF = jnp.bfloat16
F32 = jnp.float32


def shape(dims, dtype=BF):
    return jax.ShapeDtypeStruct(dims, dtype)


def call(kernel, outs, ins, mebibytes=40, scratch=()):
    tables = sum(1 for value in ins if value.dtype == jnp.int32)
    many = isinstance(outs, tuple)
    return pl.pallas_call(
        kernel,
        out_shape=outs,
        in_specs=[SMEM] * tables + [VMEM] * (len(ins) - tables),
        out_specs=(VMEM,) * len(outs) if many else VMEM,
        scratch_shapes=list(scratch),
        compiler_params=pltpu.CompilerParams(vmem_limit_bytes=mebibytes * 1024 * 1024),
    )(*ins)


def dot_t(left, right):
    return lax.dot_general(left, right, (((1,), (1,)), ((), ())), preferred_element_type=F32)


def inputs_kernel(where, leaf, mid, root, leaf_panel, mid_panel, root_panel, weights, panels):
    weights[0] = leaf[0]
    weights[1] = mid[where[0] // 2]
    weights[2] = root[...]
    panels[0] = leaf_panel[...]
    panels[1] = mid_panel[...]
    panels[2] = root_panel[...]


def fronts_kernel(where, leaf, mid, keep, give):
    first = where[1] % 2 == 0
    for kind in range(3):
        if kind == 0:
            low, high = leaf[:, :128], leaf[:, 128:]
        else:
            at = 256 * (kind - 1)
            low, high = mid[:, at : at + 128], mid[:, at + 128 : at + 256]
        keep[kind] = jnp.where(first, low, high)
        give[kind] = jnp.where(first, high, low)


def factor_kernel(
    where, leaf_fill, mid_fill, root_fill, panels, own, other,
    leaf, mid, root, stack, low, high, rows, weights,
):
    cube, row = where[0], where[1]
    first = row % 2 == 0
    fills = (
        leaf_fill[cube, row],
        mid_fill[cube // 2, 16 * (cube % 2) + row],
        root_fill[16 * cube + row],
    )
    for front, target in enumerate((leaf, mid, root)):
        for at in range(8):
            span = slice(128 * at, 128 * at + 128)
            rows[front, :, span] = panels[at, front]
            mine, theirs = own[at, front], other[at, front]
            weights[front, :64, span] = jnp.where(first, mine, theirs)
            weights[front, 64:, span] = jnp.where(first, theirs, mine)
        total = dot_t(rows[front], weights[front])
        value = (total * fills[front].astype(F32)).astype(BF)
        target[...] = value
        stack[front] = value
        low[front] = value[:128]
        high[front] = value[128:]


def turn_kernel(where, low, high, kept, cross):
    first = where[1] % 2 == 0
    for front in range(3):
        kept[front] = jnp.where(first, low[front], high[front])
    for front in range(2):
        cross[front] = jnp.where(first, low[front + 1], high[front + 1])


def columns_kernel(where, kept, partner, sent, root):
    even = where[0] % 2 == 0
    for to in range(8):
        sent[to, 0] = kept[0]
        sent[to, 1] = jnp.where(even, kept[1], partner[0])
        sent[to, 2] = jnp.where(even, partner[0], kept[1])
    root[0] = jnp.where(even, kept[2], partner[1])
    root[1] = jnp.where(even, partner[1], kept[2])


def update_kernel(
    where, own, other, blocks, own_front, other_front, out, rows, columns
):
    first, column = where[1] % 2 == 0, where[2]
    for at in range(8):
        group = (at + 8 - column) % 8
        span = slice(128 * at, 128 * at + 128)
        for front in range(2):
            mine, theirs = own[group, front], other[group, front]
            rows[front, :256, span] = jnp.where(first, mine, theirs)
            rows[front, 256:, span] = jnp.where(first, theirs, mine)
        for kind in range(3):
            columns[kind, :, span] = blocks[at, kind]
    for kind in range(3):
        product = dot_t(rows[min(kind, 1)], columns[kind])
        mine, theirs = own_front[kind], other_front[kind]
        for block in range(2):
            matrix = jnp.where(first, theirs, mine) if block else jnp.where(first, mine, theirs)
            value = matrix - product[256 * block : 256 * block + 256]
            out[:, block, kind] = value.reshape(32, 8, 128).astype(BF)


def place_kernel(where, leaf_map, mid_map, pieces, out, total):
    column = where[2]
    total[...] = jnp.zeros_like(total)
    for front in range(4):
        pair = front // 2
        slot = mid_map[pair, leaf_map[front, column]] // 16
        for block in range(16):
            target = mid_map[pair, leaf_map[front, block]]
            piece = pieces[8 * front + block // 2, block % 2, 0]
            total[4 * target + slot] += piece.astype(F32)
    for pair in range(2):
        slots = [mid_map[pair, 16 * at + column] // 16 for at in range(2)]
        for block in range(32):
            target = mid_map[pair, block]
            for at in range(2):
                piece = pieces[16 * pair + block // 2, block % 2, 1 + at]
                total[4 * target + slots[at]] += piece.astype(F32)
    out[...] = total[...].reshape(64, 4, 8, 128).astype(BF)


def root_kernel(where, factors, blocks, front, out, rows, columns):
    column = where[2]

    @pl.when(pl.program_id(0) == 0)
    def _():
        for at in range(8):
            rows[:, 128 * at : 128 * at + 128] = factors[(at + 8 - column) % 8, 0]

    for at in range(8):
        span = slice(128 * at, 128 * at + 128)
        columns[:128, span] = blocks[2 * at, 0]
        columns[128:, span] = blocks[2 * at + 1, 0]
    out[...] = front[...] - dot_t(rows[...], columns[...])


def add_kernel(base, arrived, out):
    for side in range(2):
        added = arrived[:, side, 0].astype(F32).reshape(256, 128)
        span = slice(128 * side, 128 * side + 128)
        out[:, span] = base[:, span] + added


def swap(value, axis):
    return lax.ppermute(value, axis, [(0, 1), (1, 0)])


def transpose(low, high):
    pairs = [[], []]
    for r in range(8):
        for c in range(8):
            for half in range(2):
                pairs[half].append((8 * r + c, 8 * (2 * ((c + r) % 8) + half) + r))
    plane = ROW + COL
    return lax.ppermute(low, plane, pairs[0]), lax.ppermute(high, plane, pairs[1])


def turn_weights(value):
    pairs = [(8 * q + c, 8 * (2 * c + q % 2) + q // 2) for q in range(16) for c in range(8)]
    return lax.ppermute(value, ROW + COL, pairs)


def exchange(value, axes):
    return lax.all_to_all(value, axes, 0, 0, tiled=True)


def local(
    leaf_front,
    leaf_panel,
    leaf_inverse,
    leaf_fill,
    mid_front,
    mid_panel,
    mid_inverse,
    mid_fill,
    root_front,
    root_panel,
    root_inverse,
    root_fill,
    leaf_map,
    mid_map,
):
    where = jnp.stack([lax.axis_index(CUBE), lax.axis_index(ROW), lax.axis_index(COL)])
    where = where.astype(jnp.int32)
    piece, one = shape((256, 128)), shape((128, 128))
    two, three = shape((2, 128, 128)), shape((3, 128, 128))

    weights, panels = call(
        inputs_kernel,
        (shape((3, 64, 128)), shape((3, 256, 128))),
        (where, leaf_inverse, mid_inverse, root_inverse, leaf_panel, mid_panel, root_panel),
        60,
    )
    panels = lax.all_gather(panels, COL, axis=0, tiled=False)
    weights = turn_weights(weights)
    own = exchange(jnp.broadcast_to(weights[None], (8, 3, 64, 128)), "z")
    other = swap(own, "core")
    half_front = shape((3, 256, 128), F32)
    own_front, give_front = call(
        fronts_kernel, (half_front, half_front), (where, leaf_front, mid_front)
    )
    other_front = swap(give_front, "core")
    leaf_factor, mid_factor, root_factor, stack, low, high = call(
        factor_kernel,
        (piece, piece, piece, shape((3, 256, 128)), three, three),
        (where, leaf_fill, mid_fill, root_fill, panels, own, other),
        scratch=(pltpu.VMEM((3, 256, 1024), BF), pltpu.VMEM((3, 128, 1024), BF)),
    )

    factors = lax.all_gather(stack, COL, axis=0, tiled=False)
    low, high = transpose(low, high)
    kept, cross = call(turn_kernel, (three, two), (where, low, high))
    partner = swap(cross, "half")
    sent, root_pair = call(
        columns_kernel, (shape((8, 3, 128, 128)), two), (where, kept, partner)
    )
    blocks = exchange(sent, "z")
    factors, blocks = lax.optimization_barrier((factors, blocks))
    root_other = swap(root_pair, "pair")
    root_four = jnp.where(
        lax.axis_index("pair") == 0,
        jnp.concatenate([root_pair, root_other]),
        jnp.concatenate([root_other, root_pair]),
    )
    root_blocks = lax.all_gather(root_four, ROW, axis=0, tiled=False)
    other_factors = swap(factors, "core")
    updates = call(
        update_kernel,
        shape((32, 2, 3, 8, 128)),
        (where, factors, other_factors, blocks, own_front, other_front),
        scratch=(pltpu.VMEM((2, 512, 1024), BF), pltpu.VMEM((3, 128, 1024), BF)),
    )
    pieces = exchange(updates, CUBE + ("z",))
    placed = call(
        place_kernel,
        shape((64, 4, 8, 128)),
        (where, leaf_map, mid_map, pieces),
        scratch=(pltpu.VMEM((256, 8, 128), F32),),
    )
    arrived = exchange(placed, CUBE + ROW)
    spot = pl.BlockSpec((256, 256), lambda s: (0, s))
    limit = pltpu.CompilerParams(vmem_limit_bytes=40 * 1024 * 1024)
    base = pl.pallas_call(
        root_kernel,
        grid=(4,),
        out_shape=shape((256, 1024), F32),
        in_specs=[
            SMEM,
            pl.BlockSpec((8, 1, 256, 128), lambda s: (0, 2, 0, 0)),
            pl.BlockSpec((16, 1, 128, 128), lambda s: (0, s, 0, 0)),
            spot,
        ],
        out_specs=spot,
        scratch_shapes=[pltpu.VMEM((256, 1024), BF), pltpu.VMEM((256, 1024), BF)],
        compiler_params=limit,
        cost_estimate=pl.CostEstimate(flops=2**29, bytes_accessed=2**22, transcendentals=0),
    )(where, factors, root_blocks, root_front)
    root_update = pl.pallas_call(
        add_kernel,
        grid=(4,),
        out_shape=shape((256, 1024), F32),
        in_specs=[spot, pl.BlockSpec((32, 2, 1, 8, 128), lambda s: (0, 0, s, 0, 0))],
        out_specs=spot,
        compiler_params=limit,
    )(base, arrived.reshape(32, 2, 4, 8, 128))
    return leaf_factor, mid_factor, root_factor, root_update


def solution(mesh):
    fine = Mesh(
        mesh.devices.reshape(2, 2, 8, 2, 2, 4), ("pair", "half", "z", "core", "ylo", "x")
    )
    block = P(CUBE + ROW, COL)
    in_specs = (
        block,
        block,
        P(CUBE, ROW, COL),
        P(),
        block,
        block,
        P(None, ROW, COL),
        P(),
        block,
        block,
        P(ROW, COL),
        P(),
        P(),
        P(),
    )
    return jax.shard_map(
        local, mesh=fine, in_specs=in_specs, out_specs=(block,) * 4, check_vma=False
    )
```

```python
import jax
import jax.numpy as jnp
from jax import lax
from jax.experimental import pallas as pl
from jax.experimental.pallas import tpu as pltpu
from jax.sharding import Mesh, PartitionSpec as P

CUBE = ("pair", "half")
ROW = ("z", "core")
COL = ("ylo", "x")
VMEM = pl.BlockSpec(memory_space=pltpu.VMEM)
SMEM = pl.BlockSpec(memory_space=pltpu.SMEM)
BF = jnp.bfloat16
F32 = jnp.float32


def shape(dims, dtype=BF):
    return jax.ShapeDtypeStruct(dims, dtype)


def call(kernel, outs, ins, mebibytes=40, scratch=()):
    tables = sum(1 for value in ins if value.dtype == jnp.int32)
    many = isinstance(outs, tuple)
    return pl.pallas_call(
        kernel,
        out_shape=outs,
        in_specs=[SMEM] * tables + [VMEM] * (len(ins) - tables),
        out_specs=(VMEM,) * len(outs) if many else VMEM,
        scratch_shapes=list(scratch),
        compiler_params=pltpu.CompilerParams(vmem_limit_bytes=mebibytes * 1024 * 1024),
    )(*ins)


def dot_t(left, right):
    return lax.dot_general(left, right, (((1,), (1,)), ((), ())), preferred_element_type=F32)


def inputs_kernel(
    where, leaf, mid, root, leaf_panel, mid_panel, root_panel, weights, panels, low, high
):
    for to in range(8):
        weights[to, 0] = leaf[0]
        weights[to, 1] = mid[where[0] // 2]
        weights[to, 2] = root[...]
    for front, panel in enumerate((leaf_panel, mid_panel, root_panel)):
        panels[front] = panel[...]
        low[front] = panel[:128]
        high[front] = panel[128:]


def fronts_kernel(where, leaf, mid, keep, give):
    first = where[1] % 2 == 0
    for kind in range(3):
        if kind == 0:
            low, high = leaf[:, :128], leaf[:, 128:]
        else:
            at = 256 * (kind - 1)
            low, high = mid[:, at : at + 128], mid[:, at + 128 : at + 256]
        keep[kind] = jnp.where(first, low, high)
        give[kind] = jnp.where(first, high, low)


def whole_kernel(
    where, weights, panels, low, high, whole, root, kept, cross, last, spread
):
    first = where[1] % 2 == 0
    for front in range(2):
        for at in range(8):
            whole[front, :, 128 * at : 128 * at + 128] = weights[at, front]
    for at in range(8):
        root[at] = weights[at, 2]
        spread[at] = panels[...]
    for front in range(3):
        kept[front] = jnp.where(first, low[front], high[front])
    for front in range(2):
        cross[front] = jnp.where(first, low[front + 1], high[front + 1])
    last[...] = kept[2]


def columns_kernel(
    where, kept, partner, across, corner, weights, panels, sent, joined, give
):
    cube = where[0]
    even = cube % 2 == 0
    for to in range(8):
        sent[to, 0] = kept[0]
        sent[to, 1] = jnp.where(even, kept[1], partner[0])
        sent[to, 2] = jnp.where(even, partner[0], kept[1])
    joined[:8] = weights[...]
    for slot in range(4):
        same_half, same_pair = cube % 2 == slot % 2, cube // 2 == slot // 2
        piece = jnp.where(
            same_pair,
            jnp.where(same_half, kept[2], partner[1]),
            jnp.where(same_half, across[...], corner[...]),
        )
        for half in range(2):
            joined[8 + 2 * slot + half] = piece[64 * half : 64 * half + 64]
    give[...] = panels[:, :2]


def update_kernel(
    where, leaf_fill, mid_fill, weights, own, other, blocks, own_front, other_front,
    out, leaf_factor, mid_factor, panel, factor,
):
    cube, row, column = where[0], where[1], where[2]
    first = row % 2 == 0
    upper = row - row % 2
    mine_at = pl.ds(pl.multiple_of(128 * column, 128), 128)
    for front, target in enumerate((leaf_factor, mid_factor)):
        if front == 0:
            fills = [leaf_fill[cube, upper], leaf_fill[cube, upper + 1], leaf_fill[cube, column]]
        else:
            pair, base = cube // 2, 16 * (cube % 2) + upper
            fills = [mid_fill[pair, base], mid_fill[pair, base + 1]]
            fills += [mid_fill[pair, column], mid_fill[pair, 16 + column]]
        height = 640 + 128 * front
        for at in range(8):
            span = slice(128 * at, 128 * at + 128)
            mine, theirs = own[at, front], other[at, front]
            panel[:256, span] = jnp.where(first, mine, theirs)
            panel[256:512, span] = jnp.where(first, theirs, mine)
            for kind in range(1 + front):
                piece = blocks[(at + column) % 8, kind + front]
                panel[512 + 128 * kind : 640 + 128 * kind, span] = piece
        for at in range(0, 16, 4):
            rows = weights[at : at + 4, front].reshape(256, 1024)
            part = dot_t(panel[:height], rows)
            span = slice(64 * at, 64 * at + 256)
            for index, fill in enumerate(fills):
                low = 256 * index if index < 2 else 128 * index + 256
                high = low + 256 if index < 2 else low + 128
                value = part[low:high] * fill.astype(F32)
                factor[low:high, span] = value.astype(BF)
        target[...] = jnp.where(first, factor[:256, mine_at], factor[256:512, mine_at])
        for kind in range(1 + front):
            at = kind + front
            product = dot_t(factor[:512], factor[512 + 128 * kind : 640 + 128 * kind])
            mine, theirs = own_front[at], other_front[at]
            for block in range(2):
                matrix = jnp.where(first, theirs, mine) if block else jnp.where(first, mine, theirs)
                value = matrix - product[256 * block : 256 * block + 256]
                out[:, block, at] = value.reshape(32, 8, 128).astype(BF)


def place_kernel(where, leaf_map, mid_map, pieces, out, total):
    column = where[2]
    total[...] = jnp.zeros_like(total)
    for front in range(4):
        pair = front // 2
        slot = mid_map[pair, leaf_map[front, column]] // 16
        for block in range(16):
            target = mid_map[pair, leaf_map[front, block]]
            piece = pieces[8 * front + block // 2, block % 2, 0]
            total[4 * target + slot] += piece.astype(F32)
    for pair in range(2):
        slots = [mid_map[pair, 16 * at + column] // 16 for at in range(2)]
        for block in range(32):
            target = mid_map[pair, block]
            for at in range(2):
                piece = pieces[16 * pair + block // 2, block % 2, 1 + at]
                total[4 * target + slots[at]] += piece.astype(F32)
    out[...] = total[...].reshape(64, 4, 8, 128).astype(BF)


def root_kernel(
    where, fill, panels, joined, front, out, root_factor, weights, panel, rows, columns
):
    cube, row, column = where[0], where[1], where[2]
    slot = pl.program_id(0)

    @pl.when(slot == 0)
    def _():
        for at in range(8):
            span = slice(128 * at, 128 * at + 128)
            panel[:, span] = panels[at, 0]
            for owner in range(16):
                weights[64 * owner : 64 * owner + 64, span] = joined[owner, at]
        for at in range(0, 1024, 256):
            part = dot_t(panel[...], weights[at : at + 256])
            rows[:, at : at + 256] = (part * fill[16 * cube + row].astype(F32)).astype(BF)
        root_factor[...] = rows[:, pl.ds(pl.multiple_of(128 * column, 128), 128)]

    for half in range(2):
        for at in range(8):
            owner = 2 * ((at + column) % 8) + half
            piece = joined[owner, pl.ds(8 + 2 * slot, 2)].reshape(128, 128)
            panel[128 * half : 128 * half + 128, 128 * at : 128 * at + 128] = piece
    for at in range(0, 1024, 256):
        part = dot_t(panel[...], weights[at : at + 256])
        columns[:, at : at + 256] = (part * fill[16 * slot + column].astype(F32)).astype(BF)
    out[...] = front[...] - dot_t(rows[...], columns[...])


def add_kernel(base, arrived, out):
    for side in range(2):
        added = arrived[:, side, 0].astype(F32).reshape(256, 128)
        span = slice(128 * side, 128 * side + 128)
        out[:, span] = base[:, span] + added


def swap(value, axis):
    return lax.ppermute(value, axis, [(0, 1), (1, 0)])


def transpose(low, high):
    pairs = [[], []]
    for r in range(8):
        for c in range(8):
            for half in range(2):
                pairs[half].append((8 * r + c, 8 * (2 * ((c + r) % 8) + half) + r))
    plane = ROW + COL
    return lax.ppermute(low, plane, pairs[0]), lax.ppermute(high, plane, pairs[1])


def exchange(value, axes):
    return lax.all_to_all(value, axes, 0, 0, tiled=True)


def local(
    leaf_front,
    leaf_panel,
    leaf_inverse,
    leaf_fill,
    mid_front,
    mid_panel,
    mid_inverse,
    mid_fill,
    root_front,
    root_panel,
    root_inverse,
    root_fill,
    leaf_map,
    mid_map,
):
    where = jnp.stack([lax.axis_index(CUBE), lax.axis_index(ROW), lax.axis_index(COL)])
    where = where.astype(jnp.int32)
    piece = shape((256, 128))
    two, three = shape((2, 128, 128)), shape((3, 128, 128))
    panel_three, panel_all = shape((3, 256, 128)), shape((8, 3, 256, 128))

    weights, panels, low, high = call(
        inputs_kernel,
        (shape((8, 3, 64, 128)), panel_three, three, three),
        (where, leaf_inverse, mid_inverse, root_inverse, leaf_panel, mid_panel, root_panel),
        60,
    )
    low, high = transpose(low, high)
    weights = exchange(weights, COL)
    whole, root_weights, kept, cross, last, spread = call(
        whole_kernel,
        (shape((2, 64, 1024)), shape((8, 64, 128)), three, two, shape((128, 128)), panel_all),
        (where, weights, panels, low, high),
    )
    weights = lax.all_gather(whole, ROW, axis=0, tiled=False)
    partner = swap(cross, "half")
    across = swap(last, "pair")
    corner = lax.ppermute(last, CUBE, [(0, 3), (1, 2), (2, 1), (3, 0)])
    panels = exchange(spread, COL)
    sent, joined, give = call(
        columns_kernel,
        (shape((8, 3, 128, 128)), shape((16, 64, 128)), shape((8, 2, 256, 128))),
        (where, kept, partner, across, corner, root_weights, panels),
    )
    joined = lax.all_gather(joined, ROW, axis=0, tiled=False)
    other_panels = swap(give, "core")
    half_front = shape((3, 256, 128), F32)
    own_front, give_front = call(
        fronts_kernel, (half_front, half_front), (where, leaf_front, mid_front)
    )
    other_front = swap(give_front, "core")
    blocks = exchange(sent, "z")
    blocks, other_panels, other_front = lax.optimization_barrier(
        (blocks, other_panels, other_front)
    )
    updates, leaf_factor, mid_factor = call(
        update_kernel,
        (shape((32, 2, 3, 8, 128)), piece, piece),
        (where, leaf_fill, mid_fill, weights, panels, other_panels, blocks, own_front, other_front),
        scratch=(pltpu.VMEM((768, 1024), BF), pltpu.VMEM((768, 1024), BF)),
    )
    pieces = exchange(updates, CUBE + ("z",))
    placed = call(
        place_kernel,
        shape((64, 4, 8, 128)),
        (where, leaf_map, mid_map, pieces),
        scratch=(pltpu.VMEM((256, 8, 128), F32),),
    )
    arrived = exchange(placed, CUBE + ROW)
    spot = pl.BlockSpec((256, 256), lambda s: (0, s))
    limit = pltpu.CompilerParams(vmem_limit_bytes=40 * 1024 * 1024)
    base, root_factor = pl.pallas_call(
        root_kernel,
        grid=(4,),
        out_shape=(shape((256, 1024), F32), piece),
        in_specs=[
            SMEM,
            SMEM,
            pl.BlockSpec((8, 1, 256, 128), lambda s: (0, 2, 0, 0)),
            pl.BlockSpec((16, 16, 64, 128), lambda s: (0, 0, 0, 0)),
            spot,
        ],
        out_specs=(spot, pl.BlockSpec((256, 128), lambda s: (0, 0))),
        scratch_shapes=[
            pltpu.VMEM((1024, 1024), BF),
            pltpu.VMEM((256, 1024), BF),
            pltpu.VMEM((256, 1024), BF),
            pltpu.VMEM((256, 1024), BF),
        ],
        compiler_params=limit,
        cost_estimate=pl.CostEstimate(flops=2**32, bytes_accessed=2**23, transcendentals=0),
    )(where, root_fill, panels, joined, root_front)
    root_update = pl.pallas_call(
        add_kernel,
        grid=(4,),
        out_shape=shape((256, 1024), F32),
        in_specs=[spot, pl.BlockSpec((32, 2, 1, 8, 128), lambda s: (0, 0, s, 0, 0))],
        out_specs=spot,
        compiler_params=limit,
    )(base, arrived.reshape(32, 2, 4, 8, 128))
    return leaf_factor, mid_factor, root_factor, root_update


def solution(mesh):
    fine = Mesh(
        mesh.devices.reshape(2, 2, 8, 2, 2, 4), ("pair", "half", "z", "core", "ylo", "x")
    )
    block = P(CUBE + ROW, COL)
    in_specs = (
        block,
        block,
        P(CUBE, ROW, COL),
        P(),
        block,
        block,
        P(None, ROW, COL),
        P(),
        block,
        block,
        P(ROW, COL),
        P(),
        P(),
        P(),
    )
    return jax.shard_map(
        local, mesh=fine, in_specs=in_specs, out_specs=(block,) * 4, check_vma=False
    )
```

```python
import jax
import jax.numpy as jnp
from jax import lax
from jax.experimental import pallas as pl
from jax.experimental.pallas import tpu as pltpu
from jax.sharding import Mesh, PartitionSpec as P

CUBE = ("pair", "half")
ROW = ("z", "core")
COL = ("ylo", "x")
VMEM = pl.BlockSpec(memory_space=pltpu.VMEM)
SMEM = pl.BlockSpec(memory_space=pltpu.SMEM)
ANY = pl.BlockSpec(memory_space=pl.ANY)
BF = jnp.bfloat16
F32 = jnp.float32


def shape(dims, dtype=BF):
    return jax.ShapeDtypeStruct(dims, dtype)


def call(kernel, outs, ins, mebibytes=20, scratch=(), after=(), cost=None):
    tables = sum(1 for value in ins if value.dtype == jnp.int32)
    many = isinstance(outs, tuple)
    return pl.pallas_call(
        kernel,
        out_shape=outs,
        in_specs=[SMEM] * tables + [VMEM] * (len(ins) - tables) + [ANY] * len(after),
        out_specs=(VMEM,) * len(outs) if many else VMEM,
        scratch_shapes=list(scratch),
        compiler_params=pltpu.CompilerParams(vmem_limit_bytes=mebibytes * 1024 * 1024),
        cost_estimate=cost and pl.CostEstimate(cost[0], 0, cost[1]),
    )(*ins, *after)


def cube_at():
    return lax.axis_index(CUBE)


def row_at():
    return lax.axis_index(ROW)


def column_at():
    return lax.axis_index(COL)


def dot_t(left, right):
    return lax.dot_general(left, right, (((1,), (1,)), ((), ())), preferred_element_type=F32)


def inputs_kernel(
    leaf, mid, root, leaf_panel, mid_panel, root_panel, weights, spread, low, high
):
    for to in range(8):
        weights[to, 0] = leaf[0]
        weights[to, 1] = mid[cube_at() // 2]
        weights[to, 2] = root[...]
        for front, panel in enumerate((leaf_panel, mid_panel, root_panel)):
            spread[to, front] = panel[...]
    for front, panel in enumerate((leaf_panel, mid_panel, root_panel)):
        low[front] = panel[:128]
        high[front] = panel[128:]


def half_of(kind, side, leaf, mid):
    if kind == 0:
        return leaf[:, 128 * side : 128 * side + 128]
    at = 256 * (kind - 1) + 128 * side
    return mid[:, at : at + 128]


def fronts_kernel(leaf, mid, give):
    first = row_at() % 2 == 0
    for kind in range(3):
        give[kind] = jnp.where(first, half_of(kind, 1, leaf, mid), half_of(kind, 0, leaf, mid))


def whole_kernel(
    weights, low, high, whole, root, kept, cross, last
):
    first = row_at() % 2 == 0
    for front in range(2):
        for at in range(8):
            whole[front, :, 128 * at : 128 * at + 128] = weights[at, front]
    for at in range(8):
        root[at] = weights[at, 2]
    for front in range(3):
        kept[front] = jnp.where(first, low[front], high[front])
    for front in range(2):
        cross[front] = jnp.where(first, low[front + 1], high[front + 1])
    last[...] = kept[2]


def columns_kernel(
    kept, partner, across, corner, weights, _, sent, joined
):
    cube = cube_at()
    even = cube % 2 == 0
    for to in range(8):
        sent[to, 0] = kept[0]
        sent[to, 1] = jnp.where(even, kept[1], partner[0])
        sent[to, 2] = jnp.where(even, partner[0], kept[1])
    joined[:8] = weights[...]
    for slot in range(4):
        same_half, same_pair = cube % 2 == slot % 2, cube // 2 == slot // 2
        piece = jnp.where(
            same_pair,
            jnp.where(same_half, kept[2], partner[1]),
            jnp.where(same_half, across[...], corner[...]),
        )
        for half in range(2):
            joined[8 + 2 * slot + half] = piece[64 * half : 64 * half + 64]


def factor_kernel(
    leaf_fill, mid_fill, far_weights, far_own, far_other, _,
    turned, keep, give, panel, factor, total, weights, own, other, sems,
):
    cube, row, column = cube_at(), row_at(), column_at()
    front = row % 2
    first = front == 0
    upper = row - front
    pairs = ((far_own, own), (far_other, other), (far_weights, weights))
    moves = [
        pltpu.make_async_copy(far.at[:, front], near, sems.at[at])
        for at, (far, near) in enumerate(pairs)
    ]
    for move in moves:
        move.start()
    pair, base = cube // 2, 16 * (cube % 2) + upper
    fills = [
        jnp.where(first, leaf_fill[cube, upper + index], mid_fill[pair, base + index])
        for index in range(2)
    ]
    for move in moves:
        move.wait()
    for at in range(8):
        span = slice(128 * at, 128 * at + 128)
        panel[:256, span] = jnp.where(first, own[at], other[at])
        panel[256:, span] = jnp.where(first, other[at], own[at])
    for at in range(0, 16, 4):
        rows_of = weights[at : at + 4].reshape(256, 1024)
        part = dot_t(panel[...], rows_of)
        span = slice(64 * at, 64 * at + 256)
        for index, fill in enumerate(fills):
            rows = slice(256 * index, 256 * index + 256)
            factor[rows, span] = (part[rows] * fill.astype(F32)).astype(BF)
        more = jnp.dot(factor[:, span], rows_of, preferred_element_type=F32)
        total[...] = more if at == 0 else total[...] + more
    turned[...] = total[...].astype(BF)
    mine_at = pl.ds(pl.multiple_of(128 * column, 128), 128)
    keep[...] = jnp.where(first, factor[:256, mine_at], factor[256:, mine_at])
    give[...] = jnp.where(first, factor[256:, mine_at], factor[:256, mine_at])


def update_kernel(
    leaf_fill, mid_fill, turned, other_turned, blocks, leaf, mid, other_front, out, panel
):
    cube, row, column = cube_at(), row_at(), column_at()
    first = row % 2 == 0
    pair = cube // 2
    fills = [leaf_fill[cube, column], mid_fill[pair, column], mid_fill[pair, 16 + column]]
    for kind, fill in enumerate(fills):
        for at in range(8):
            panel[kind, :, 128 * at : 128 * at + 128] = blocks[(at + column) % 8, kind]
        if kind < 2:
            same = first if kind == 0 else jnp.logical_not(first)
            rows = jnp.where(same, turned[...], other_turned[...])
        product = dot_t(rows, panel[kind]) * fill.astype(F32)
        mine = jnp.where(first, half_of(kind, 0, leaf, mid), half_of(kind, 1, leaf, mid))
        theirs = other_front[kind]
        for block in range(2):
            matrix = jnp.where(first, theirs, mine) if block else jnp.where(first, mine, theirs)
            value = matrix - product[256 * block : 256 * block + 256]
            out[:, block, kind] = value.reshape(32, 8, 128).astype(BF)


def place_kernel(leaf_map, mid_map, pieces, out, total):
    column = column_at()
    total[...] = jnp.zeros_like(total)
    for front in range(4):
        pair = front // 2
        slot = mid_map[pair, leaf_map[front, column]] // 16
        for block in range(16):
            target = mid_map[pair, leaf_map[front, block]]
            piece = pieces[8 * front + block // 2, block % 2, 0]
            total[4 * target + slot] += piece.astype(F32)
    for pair in range(2):
        slots = [mid_map[pair, 16 * at + column] // 16 for at in range(2)]
        for block in range(32):
            target = mid_map[pair, block]
            for at in range(2):
                piece = pieces[16 * pair + block // 2, block % 2, 1 + at]
                total[4 * target + slots[at]] += piece.astype(F32)
    out[...] = total[...].reshape(64, 4, 8, 128).astype(BF)


def root_kernel(
    fill, panels, joined, front, out, root_factor, weights, panel, factor, turned
):
    cube, row, column = cube_at(), row_at(), column_at()
    slot = pl.program_id(0)

    @pl.when(slot == 0)
    def _():
        for at in range(8):
            span = slice(128 * at, 128 * at + 128)
            panel[:, span] = panels[at, 0]
            for owner in range(16):
                weights[64 * owner : 64 * owner + 64, span] = joined[owner, at]
        for at in range(0, 1024, 256):
            part = dot_t(panel[...], weights[at : at + 256])
            factor[:, at : at + 256] = (part * fill[16 * cube + row].astype(F32)).astype(BF)
        turned[...] = jnp.dot(factor[...], weights[...], preferred_element_type=F32).astype(BF)
        root_factor[...] = factor[:, pl.ds(pl.multiple_of(128 * column, 128), 128)]

    for half in range(2):
        for at in range(8):
            owner = 2 * ((at + column) % 8) + half
            piece = joined[owner, pl.ds(8 + 2 * slot, 2)].reshape(128, 128)
            panel[128 * half : 128 * half + 128, 128 * at : 128 * at + 128] = piece
    product = dot_t(turned[...], panel[...]) * fill[16 * slot + column].astype(F32)
    out[...] = front[...] - product


def add_kernel(base, arrived, out):
    for side in range(2):
        added = arrived[:, side, 0].astype(F32).reshape(256, 128)
        span = slice(128 * side, 128 * side + 128)
        out[:, span] = base[:, span] + added


def swap(value, axis):
    return lax.ppermute(value, axis, [(0, 1), (1, 0)])


def transpose(low, high):
    pairs = [[], []]
    for r in range(8):
        for c in range(8):
            for half in range(2):
                pairs[half].append((8 * r + c, 8 * (2 * ((c + r) % 8) + half) + r))
    plane = ROW + COL
    return lax.ppermute(low, plane, pairs[0]), lax.ppermute(high, plane, pairs[1])


def exchange(value, axes):
    return lax.all_to_all(value, axes, 0, 0, tiled=True)


def local(
    leaf_front,
    leaf_panel,
    leaf_inverse,
    leaf_fill,
    mid_front,
    mid_panel,
    mid_inverse,
    mid_fill,
    root_front,
    root_panel,
    root_inverse,
    root_fill,
    leaf_map,
    mid_map,
):
    piece = shape((256, 128))
    two, three = shape((2, 128, 128)), shape((3, 128, 128))
    panel_all = shape((8, 3, 256, 128))

    weights, spread, low, high = call(
        inputs_kernel,
        (shape((8, 3, 64, 128)), panel_all, three, three),
        (leaf_inverse, mid_inverse, root_inverse, leaf_panel, mid_panel, root_panel),
        60,
    )
    low, high = transpose(low, high)
    weights = exchange(weights, COL)
    whole, root_weights, kept, cross, last = call(
        whole_kernel,
        (shape((2, 64, 1024)), shape((8, 64, 128)), three, two, shape((128, 128))),
        (weights, low, high),
    )
    whole, spread = lax.optimization_barrier((whole, spread))
    weights = lax.all_gather(whole, ROW, axis=0, tiled=False)
    partner = swap(cross, "half")
    across = swap(last, "pair")
    corner = lax.ppermute(last, CUBE, [(0, 3), (1, 2), (2, 1), (3, 0)])
    panels = exchange(spread, COL)
    sent, joined = call(
        columns_kernel,
        (shape((8, 3, 128, 128)), shape((16, 64, 128))),
        (kept, partner, across, corner, root_weights),
        after=(panels,),
    )
    sent, joined, panels = lax.optimization_barrier((sent, joined, panels))
    joined = lax.all_gather(joined, ROW, axis=0, tiled=False)
    other_panels = swap(panels, "core")
    half_front = shape((3, 256, 128), F32)
    give_front = call(fronts_kernel, half_front, (leaf_front, mid_front))
    other_front = swap(give_front, "core")
    blocks = exchange(sent, "z")
    turned, keep, give = call(
        factor_kernel,
        (shape((512, 1024)), piece, piece),
        (leaf_fill, mid_fill),
        60,
        scratch=(
            pltpu.VMEM((512, 1024), BF),
            pltpu.VMEM((512, 1024), BF),
            pltpu.VMEM((512, 1024), F32),
            pltpu.VMEM((16, 64, 1024), BF),
            pltpu.VMEM((8, 256, 128), BF),
            pltpu.VMEM((8, 256, 128), BF),
            pltpu.SemaphoreType.DMA((3,)),
        ),
        after=(weights, panels, other_panels, other_front),
        cost=(2**31, 2**22),
    )
    other_turned = swap(turned, "core")
    blocks, other_turned = lax.optimization_barrier((blocks, other_turned))
    updates = call(
        update_kernel,
        shape((32, 2, 3, 8, 128)),
        (leaf_fill, mid_fill, turned, other_turned, blocks, leaf_front, mid_front, other_front),
        60,
        scratch=(pltpu.VMEM((3, 128, 1024), BF),),
    )
    given = swap(give, "core")
    leaf_first = lax.axis_index("core") == 0
    leaf_factor = jnp.where(leaf_first, keep, given)
    mid_factor = jnp.where(leaf_first, given, keep)
    pieces = exchange(updates, CUBE + ("z",))
    placed = call(
        place_kernel,
        shape((64, 4, 8, 128)),
        (leaf_map, mid_map, pieces),
        scratch=(pltpu.VMEM((256, 8, 128), F32),),
    )
    arrived = exchange(placed, CUBE + ROW)
    spot = pl.BlockSpec((256, 256), lambda s: (0, s))
    limit = pltpu.CompilerParams(vmem_limit_bytes=24 * 1024 * 1024)
    base, root_factor = pl.pallas_call(
        root_kernel,
        grid=(4,),
        out_shape=(shape((256, 1024), F32), piece),
        in_specs=[
            SMEM,
            pl.BlockSpec((8, 1, 256, 128), lambda s: (0, 2, 0, 0)),
            pl.BlockSpec((16, 16, 64, 128), lambda s: (0, 0, 0, 0)),
            spot,
        ],
        out_specs=(spot, pl.BlockSpec((256, 128), lambda s: (0, 0))),
        scratch_shapes=[
            pltpu.VMEM((1024, 1024), BF),
            pltpu.VMEM((256, 1024), BF),
            pltpu.VMEM((256, 1024), BF),
            pltpu.VMEM((256, 1024), BF),
        ],
        compiler_params=limit,
        cost_estimate=pl.CostEstimate(flops=2**32, bytes_accessed=2**23, transcendentals=0),
    )(root_fill, panels, joined, root_front)
    root_update = pl.pallas_call(
        add_kernel,
        grid=(4,),
        out_shape=shape((256, 1024), F32),
        in_specs=[spot, pl.BlockSpec((32, 2, 1, 8, 128), lambda s: (0, 0, s, 0, 0))],
        out_specs=spot,
        compiler_params=limit,
    )(base, arrived.reshape(32, 2, 4, 8, 128))
    return leaf_factor, mid_factor, root_factor, root_update


def solution(mesh):
    fine = Mesh(
        mesh.devices.reshape(2, 2, 8, 2, 2, 4), ("pair", "half", "z", "core", "ylo", "x")
    )
    block = P(CUBE + ROW, COL)
    in_specs = (
        block,
        block,
        P(CUBE, ROW, COL),
        P(),
        block,
        block,
        P(None, ROW, COL),
        P(),
        block,
        block,
        P(ROW, COL),
        P(),
        P(),
        P(),
    )
    return jax.shard_map(
        local, mesh=fine, in_specs=in_specs, out_specs=(block,) * 4, check_vma=False
    )
```

```python
import jax
import jax.numpy as jnp
from jax import lax
from jax.experimental import pallas as pl
from jax.experimental.pallas import tpu as pltpu
from jax.sharding import Mesh, PartitionSpec as P

CUBE = ("pair", "half")
ROW = ("z", "core")
COL = ("ylo", "x")
VMEM = pl.BlockSpec(memory_space=pltpu.VMEM)
SMEM = pl.BlockSpec(memory_space=pltpu.SMEM)
ANY = pl.BlockSpec(memory_space=pl.ANY)
BF = jnp.bfloat16
F32 = jnp.float32


def shape(dims, dtype=BF):
    return jax.ShapeDtypeStruct(dims, dtype)


def call(kernel, outs, ins, mebibytes=20, scratch=(), after=(), cost=None):
    tables = sum(1 for value in ins if value.dtype == jnp.int32)
    many = isinstance(outs, tuple)
    return pl.pallas_call(
        kernel,
        out_shape=outs,
        in_specs=[SMEM] * tables + [VMEM] * (len(ins) - tables) + [ANY] * len(after),
        out_specs=(VMEM,) * len(outs) if many else VMEM,
        scratch_shapes=list(scratch),
        compiler_params=pltpu.CompilerParams(vmem_limit_bytes=mebibytes * 1024 * 1024),
        cost_estimate=cost and pl.CostEstimate(cost[0], 0, cost[1]),
    )(*ins, *after)


def cube_at():
    return lax.axis_index(CUBE)


def row_at():
    return lax.axis_index(ROW)


def column_at():
    return lax.axis_index(COL)


def dot_t(left, right):
    return lax.dot_general(left, right, (((1,), (1,)), ((), ())), preferred_element_type=F32)


def inputs_kernel(
    leaf, mid, root, leaf_panel, mid_panel, root_panel, weights, spread, low, high
):
    for to in range(8):
        weights[to, 0] = leaf[0]
        weights[to, 1] = mid[cube_at() // 2]
        weights[to, 2] = root[...]
        for front, panel in enumerate((leaf_panel, mid_panel, root_panel)):
            spread[to, front] = panel[...]
    for front, panel in enumerate((leaf_panel, mid_panel, root_panel)):
        low[front] = panel[:128]
        high[front] = panel[128:]


def half_of(kind, side, leaf, mid):
    if kind == 0:
        return leaf[:, 128 * side : 128 * side + 128]
    at = 256 * (kind - 1) + 128 * side
    return mid[:, at : at + 128]


def fronts_kernel(leaf, mid, give):
    first = row_at() % 2 == 0
    for kind in range(3):
        give[kind] = jnp.where(first, half_of(kind, 1, leaf, mid), half_of(kind, 0, leaf, mid))


def whole_kernel(
    weights, low, high, whole, root, kept, cross, last
):
    first = row_at() % 2 == 0
    for front in range(2):
        for at in range(8):
            whole[front, :, 128 * at : 128 * at + 128] = weights[at, front]
    for at in range(8):
        root[at] = weights[at, 2]
    for front in range(3):
        kept[front] = jnp.where(first, low[front], high[front])
    for front in range(2):
        cross[front] = jnp.where(first, low[front + 1], high[front + 1])
    last[...] = kept[2]


def columns_kernel(
    kept, partner, across, corner, weights, _, sent, joined
):
    cube = cube_at()
    even = cube % 2 == 0
    for to in range(8):
        sent[to, 0] = kept[0]
        sent[to, 1] = jnp.where(even, kept[1], partner[0])
        sent[to, 2] = jnp.where(even, partner[0], kept[1])
    joined[:8] = weights[...]
    for slot in range(4):
        same_half, same_pair = cube % 2 == slot % 2, cube // 2 == slot // 2
        piece = jnp.where(
            same_pair,
            jnp.where(same_half, kept[2], partner[1]),
            jnp.where(same_half, across[...], corner[...]),
        )
        for half in range(2):
            joined[8 + 2 * slot + half] = piece[64 * half : 64 * half + 64]


def factor_kernel(
    leaf_fill, mid_fill, far_weights, far_own, far_other, _,
    turned, keep, give, panel, factor, total, weights, own, other, sems,
):
    cube, row, column = cube_at(), row_at(), column_at()
    front = row % 2
    first = front == 0
    upper = row - front
    pairs = ((far_own, own), (far_other, other), (far_weights, weights))
    moves = [
        pltpu.make_async_copy(far.at[:, front], near, sems.at[at])
        for at, (far, near) in enumerate(pairs)
    ]
    for move in moves:
        move.start()
    pair, base = cube // 2, 16 * (cube % 2) + upper
    fills = [
        jnp.where(first, leaf_fill[cube, upper + index], mid_fill[pair, base + index])
        for index in range(2)
    ]
    for move in moves:
        move.wait()
    for at in range(8):
        span = slice(128 * at, 128 * at + 128)
        panel[:256, span] = jnp.where(first, own[at], other[at])
        panel[256:, span] = jnp.where(first, other[at], own[at])
    for at in range(0, 16, 4):
        rows_of = weights[at : at + 4].reshape(256, 1024)
        part = dot_t(panel[...], rows_of)
        span = slice(64 * at, 64 * at + 256)
        for index, fill in enumerate(fills):
            rows = slice(256 * index, 256 * index + 256)
            factor[rows, span] = (part[rows] * fill.astype(F32)).astype(BF)
        more = jnp.dot(factor[:, span], rows_of, preferred_element_type=F32)
        total[...] = more if at == 0 else total[...] + more
    turned[...] = total[...].astype(BF)
    mine_at = pl.ds(pl.multiple_of(128 * column, 128), 128)
    keep[...] = jnp.where(first, factor[:256, mine_at], factor[256:, mine_at])
    give[...] = jnp.where(first, factor[256:, mine_at], factor[:256, mine_at])


def update_kernel(
    leaf_fill, mid_fill, turned, other_turned, blocks, leaf, mid, other_front, out, panel
):
    cube, row, column = cube_at(), row_at(), column_at()
    first = row % 2 == 0
    pair = cube // 2
    fills = [leaf_fill[cube, column], mid_fill[pair, column], mid_fill[pair, 16 + column]]
    for kind, fill in enumerate(fills):
        for at in range(8):
            panel[kind, :, 128 * at : 128 * at + 128] = blocks[(at + column) % 8, kind]
        if kind < 2:
            same = first if kind == 0 else jnp.logical_not(first)
            rows = jnp.where(same, turned[...], other_turned[...])
        product = dot_t(rows, panel[kind]) * fill.astype(F32)
        mine = jnp.where(first, half_of(kind, 0, leaf, mid), half_of(kind, 1, leaf, mid))
        theirs = other_front[kind]
        for block in range(2):
            matrix = jnp.where(first, theirs, mine) if block else jnp.where(first, mine, theirs)
            value = matrix - product[256 * block : 256 * block + 256]
            out[:, block, kind] = value.reshape(32, 8, 128).astype(BF)


def place_kernel(leaf_map, mid_map, pieces, out, total):
    column = column_at()
    total[...] = jnp.zeros_like(total)
    for front in range(4):
        pair = front // 2
        slot = mid_map[pair, leaf_map[front, column]] // 16
        for block in range(16):
            target = mid_map[pair, leaf_map[front, block]]
            piece = pieces[8 * front + block // 2, block % 2, 0]
            total[4 * target + slot] += piece.astype(F32)
    for pair in range(2):
        slots = [mid_map[pair, 16 * at + column] // 16 for at in range(2)]
        for block in range(32):
            target = mid_map[pair, block]
            for at in range(2):
                piece = pieces[16 * pair + block // 2, block % 2, 1 + at]
                total[4 * target + slots[at]] += piece.astype(F32)
    out[...] = total[...].reshape(64, 4, 8, 128).astype(BF)


def root_kernel(
    fill, panels, joined, front, out, root_factor, weights, panel, factor, turned
):
    cube, row, column = cube_at(), row_at(), column_at()
    slot = pl.program_id(0)

    @pl.when(slot == 0)
    def _():
        for at in range(8):
            span = slice(128 * at, 128 * at + 128)
            panel[:, span] = panels[at, 0]
            for owner in range(16):
                weights[64 * owner : 64 * owner + 64, span] = joined[owner, at]
        for at in range(0, 1024, 256):
            part = dot_t(panel[...], weights[at : at + 256])
            factor[:, at : at + 256] = (part * fill[16 * cube + row].astype(F32)).astype(BF)
        turned[...] = jnp.dot(factor[...], weights[...], preferred_element_type=F32).astype(BF)
        root_factor[...] = factor[:, pl.ds(pl.multiple_of(128 * column, 128), 128)]

    for half in range(2):
        for at in range(8):
            owner = 2 * ((at + column) % 8) + half
            piece = joined[owner, pl.ds(8 + 2 * slot, 2)].reshape(128, 128)
            panel[128 * half : 128 * half + 128, 128 * at : 128 * at + 128] = piece
    product = dot_t(turned[...], panel[...]) * fill[16 * slot + column].astype(F32)
    out[...] = front[...] - product


def add_kernel(base, arrived, out):
    for side in range(2):
        added = arrived[:, side, 0].astype(F32).reshape(256, 128)
        span = slice(128 * side, 128 * side + 128)
        out[:, span] = base[:, span] + added


def swap(value, axis):
    return lax.ppermute(value, axis, [(0, 1), (1, 0)])


def transpose(low, high):
    pairs = [[], []]
    for r in range(8):
        for c in range(8):
            for half in range(2):
                pairs[half].append((8 * r + c, 8 * (2 * ((c + r) % 8) + half) + r))
    plane = ROW + COL
    return lax.ppermute(low, plane, pairs[0]), lax.ppermute(high, plane, pairs[1])


def exchange(value, axes):
    return lax.all_to_all(value, axes, 0, 0, tiled=True)


def local(
    leaf_front,
    leaf_panel,
    leaf_inverse,
    leaf_fill,
    mid_front,
    mid_panel,
    mid_inverse,
    mid_fill,
    root_front,
    root_panel,
    root_inverse,
    root_fill,
    leaf_map,
    mid_map,
):
    piece = shape((256, 128))
    two, three = shape((2, 128, 128)), shape((3, 128, 128))
    panel_all = shape((8, 3, 256, 128))

    weights, spread, low, high = call(
        inputs_kernel,
        (shape((8, 3, 64, 128)), panel_all, three, three),
        (leaf_inverse, mid_inverse, root_inverse, leaf_panel, mid_panel, root_panel),
        60,
    )
    low, high = transpose(low, high)
    weights = exchange(weights, COL)
    whole, root_weights, kept, cross, last = call(
        whole_kernel,
        (shape((2, 64, 1024)), shape((8, 64, 128)), three, two, shape((128, 128))),
        (weights, low, high),
    )
    whole, spread = lax.optimization_barrier((whole, spread))
    weights = lax.all_gather(whole, ROW, axis=0, tiled=False)
    partner = swap(cross, "half")
    across = swap(last, "pair")
    corner = lax.ppermute(last, CUBE, [(0, 3), (1, 2), (2, 1), (3, 0)])
    panels = exchange(spread, COL)
    sent, joined = call(
        columns_kernel,
        (shape((8, 3, 128, 128)), shape((16, 64, 128))),
        (kept, partner, across, corner, root_weights),
        after=(panels,),
    )
    sent, joined, panels = lax.optimization_barrier((sent, joined, panels))
    joined = lax.all_gather(joined, ROW, axis=0, tiled=False)
    other_panels = swap(panels, "core")
    half_front = shape((3, 256, 128), F32)
    give_front = call(fronts_kernel, half_front, (leaf_front, mid_front))
    other_front = swap(give_front, "core")
    blocks = exchange(sent, "z")
    turned, keep, give = call(
        factor_kernel,
        (shape((512, 1024)), piece, piece),
        (leaf_fill, mid_fill),
        60,
        scratch=(
            pltpu.VMEM((512, 1024), BF),
            pltpu.VMEM((512, 1024), BF),
            pltpu.VMEM((512, 1024), F32),
            pltpu.VMEM((16, 64, 1024), BF),
            pltpu.VMEM((8, 256, 128), BF),
            pltpu.VMEM((8, 256, 128), BF),
            pltpu.SemaphoreType.DMA((3,)),
        ),
        after=(weights, panels, other_panels, other_front),
        cost=(2**31, 2**22),
    )
    other_turned = swap(turned, "core")
    blocks, other_turned = lax.optimization_barrier((blocks, other_turned))
    updates = call(
        update_kernel,
        shape((32, 2, 3, 8, 128)),
        (leaf_fill, mid_fill, turned, other_turned, blocks, leaf_front, mid_front, other_front),
        44,
        scratch=(pltpu.VMEM((3, 128, 1024), BF),),
    )
    given = swap(give, "core")
    leaf_first = lax.axis_index("core") == 0
    leaf_factor = jnp.where(leaf_first, keep, given)
    mid_factor = jnp.where(leaf_first, given, keep)
    pieces = exchange(updates, CUBE + ("z",))
    placed = call(
        place_kernel,
        shape((64, 4, 8, 128)),
        (leaf_map, mid_map, pieces),
        scratch=(pltpu.VMEM((256, 8, 128), F32),),
    )
    arrived = exchange(placed, CUBE + ROW)
    spot = pl.BlockSpec((256, 256), lambda s: (0, s))
    limit = pltpu.CompilerParams(vmem_limit_bytes=24 * 1024 * 1024)
    base, root_factor = pl.pallas_call(
        root_kernel,
        grid=(4,),
        out_shape=(shape((256, 1024), F32), piece),
        in_specs=[
            SMEM,
            pl.BlockSpec((8, 1, 256, 128), lambda s: (0, 2, 0, 0)),
            pl.BlockSpec((16, 16, 64, 128), lambda s: (0, 0, 0, 0)),
            spot,
        ],
        out_specs=(spot, pl.BlockSpec((256, 128), lambda s: (0, 0))),
        scratch_shapes=[
            pltpu.VMEM((1024, 1024), BF),
            pltpu.VMEM((256, 1024), BF),
            pltpu.VMEM((256, 1024), BF),
            pltpu.VMEM((256, 1024), BF),
        ],
        compiler_params=limit,
        cost_estimate=pl.CostEstimate(flops=2**32, bytes_accessed=2**23, transcendentals=0),
    )(root_fill, panels, joined, root_front)
    root_update = pl.pallas_call(
        add_kernel,
        grid=(4,),
        out_shape=shape((256, 1024), F32),
        in_specs=[spot, pl.BlockSpec((32, 2, 1, 8, 128), lambda s: (0, 0, s, 0, 0))],
        out_specs=spot,
        compiler_params=limit,
    )(base, arrived.reshape(32, 2, 4, 8, 128))
    return leaf_factor, mid_factor, root_factor, root_update


def solution(mesh):
    fine = Mesh(
        mesh.devices.reshape(2, 2, 8, 2, 2, 4), ("pair", "half", "z", "core", "ylo", "x")
    )
    block = P(CUBE + ROW, COL)
    in_specs = (
        block,
        block,
        P(CUBE, ROW, COL),
        P(),
        block,
        block,
        P(None, ROW, COL),
        P(),
        block,
        block,
        P(ROW, COL),
        P(),
        P(),
        P(),
    )
    return jax.shard_map(
        local, mesh=fine, in_specs=in_specs, out_specs=(block,) * 4, check_vma=False
    )
```

```python
import jax
import jax.numpy as jnp
from jax import lax
from jax.experimental import pallas as pl
from jax.experimental.pallas import tpu as pltpu
from jax.sharding import Mesh, PartitionSpec as P

CUBE = ("pair", "half")
ROW = ("z", "core")
COL = ("ylo", "x")
VMEM = pl.BlockSpec(memory_space=pltpu.VMEM)
SMEM = pl.BlockSpec(memory_space=pltpu.SMEM)
ANY = pl.BlockSpec(memory_space=pl.ANY)
BF = jnp.bfloat16
F32 = jnp.float32


def shape(dims, dtype=BF):
    return jax.ShapeDtypeStruct(dims, dtype)


def call(kernel, outs, ins, mebibytes=20, scratch=(), after=(), cost=None):
    tables = sum(1 for value in ins if value.dtype == jnp.int32)
    many = isinstance(outs, tuple)
    return pl.pallas_call(
        kernel,
        out_shape=outs,
        in_specs=[SMEM] * tables + [VMEM] * (len(ins) - tables) + [ANY] * len(after),
        out_specs=(VMEM,) * len(outs) if many else VMEM,
        scratch_shapes=list(scratch),
        compiler_params=pltpu.CompilerParams(vmem_limit_bytes=mebibytes * 1024 * 1024),
        cost_estimate=cost and pl.CostEstimate(cost[0], 0, cost[1]),
    )(*ins, *after)


def cube_at():
    return lax.axis_index(CUBE)


def row_at():
    return lax.axis_index(ROW)


def column_at():
    return lax.axis_index(COL)


def dot_t(left, right):
    return lax.dot_general(left, right, (((1,), (1,)), ((), ())), preferred_element_type=F32)


def inputs_kernel(
    leaf, mid, root, leaf_panel, mid_panel, root_panel, weights, spread, low, high
):
    for to in range(8):
        weights[to, 0] = leaf[0]
        weights[to, 1] = mid[cube_at() // 2]
        weights[to, 2] = root[...]
        for front, panel in enumerate((leaf_panel, mid_panel, root_panel)):
            spread[to, front] = panel[...]
    for front, panel in enumerate((leaf_panel, mid_panel, root_panel)):
        low[front] = panel[:128]
        high[front] = panel[128:]


def half_of(kind, side, leaf, mid):
    if kind == 0:
        return leaf[:, 128 * side : 128 * side + 128]
    at = 256 * (kind - 1) + 128 * side
    return mid[:, at : at + 128]


def fronts_kernel(leaf, mid, give):
    first = row_at() % 2 == 0
    for kind in range(3):
        give[kind] = jnp.where(first, half_of(kind, 1, leaf, mid), half_of(kind, 0, leaf, mid))


def whole_kernel(
    weights, low, high, whole, root, kept, cross, last
):
    first = row_at() % 2 == 0
    for front in range(2):
        for at in range(8):
            whole[front, :, 128 * at : 128 * at + 128] = weights[at, front]
    for at in range(8):
        root[at] = weights[at, 2]
    for front in range(3):
        kept[front] = jnp.where(first, low[front], high[front])
    for front in range(2):
        cross[front] = jnp.where(first, low[front + 1], high[front + 1])
    last[...] = kept[2]


def columns_kernel(
    kept, partner, across, corner, weights, _, sent, joined
):
    cube = cube_at()
    even = cube % 2 == 0
    for to in range(8):
        sent[to, 0] = kept[0]
        sent[to, 1] = jnp.where(even, kept[1], partner[0])
        sent[to, 2] = jnp.where(even, partner[0], kept[1])
    joined[:8] = weights[...]
    for slot in range(4):
        same_half, same_pair = cube % 2 == slot % 2, cube // 2 == slot // 2
        piece = jnp.where(
            same_pair,
            jnp.where(same_half, kept[2], partner[1]),
            jnp.where(same_half, across[...], corner[...]),
        )
        for half in range(2):
            joined[8 + 2 * slot + half] = piece[64 * half : 64 * half + 64]


def factor_kernel(
    leaf_fill, mid_fill, far_weights, far_own, far_other, _,
    turned, keep, give, panel, factor, total, weights, own, other, sems,
):
    cube, row, column = cube_at(), row_at(), column_at()
    front = row % 2
    first = front == 0
    upper = row - front
    pairs = ((far_own, own), (far_other, other), (far_weights, weights))
    moves = [
        pltpu.make_async_copy(far.at[:, front], near, sems.at[at])
        for at, (far, near) in enumerate(pairs)
    ]
    for move in moves:
        move.start()
    pair, base = cube // 2, 16 * (cube % 2) + upper
    fills = [
        jnp.where(first, leaf_fill[cube, upper + index], mid_fill[pair, base + index])
        for index in range(2)
    ]
    for move in moves:
        move.wait()
    for at in range(8):
        span = slice(128 * at, 128 * at + 128)
        panel[:256, span] = jnp.where(first, own[at], other[at])
        panel[256:, span] = jnp.where(first, other[at], own[at])
    for at in range(0, 16, 4):
        rows_of = weights[at : at + 4].reshape(256, 1024)
        part = dot_t(panel[...], rows_of)
        span = slice(64 * at, 64 * at + 256)
        for index, fill in enumerate(fills):
            rows = slice(256 * index, 256 * index + 256)
            factor[rows, span] = (part[rows] * fill.astype(F32)).astype(BF)
        more = jnp.dot(factor[:, span], rows_of, preferred_element_type=F32)
        total[...] = more if at == 0 else total[...] + more
    turned[...] = total[...].astype(BF)
    mine_at = pl.ds(pl.multiple_of(128 * column, 128), 128)
    keep[...] = jnp.where(first, factor[:256, mine_at], factor[256:, mine_at])
    give[...] = jnp.where(first, factor[256:, mine_at], factor[:256, mine_at])


def update_kernel(
    leaf_fill, mid_fill, turned, other_turned, blocks, leaf, mid, other_front, out, panel
):
    cube, row, column = cube_at(), row_at(), column_at()
    first = row % 2 == 0
    pair = cube // 2
    fills = [leaf_fill[cube, column], mid_fill[pair, column], mid_fill[pair, 16 + column]]
    for kind, fill in enumerate(fills):
        for at in range(8):
            panel[kind, :, 128 * at : 128 * at + 128] = blocks[(at + column) % 8, kind]
        if kind < 2:
            same = first if kind == 0 else jnp.logical_not(first)
            rows = jnp.where(same, turned[...], other_turned[...])
        product = dot_t(rows, panel[kind]) * fill.astype(F32)
        mine = jnp.where(first, half_of(kind, 0, leaf, mid), half_of(kind, 1, leaf, mid))
        theirs = other_front[kind]
        for block in range(2):
            matrix = jnp.where(first, theirs, mine) if block else jnp.where(first, mine, theirs)
            value = matrix - product[256 * block : 256 * block + 256]
            out[:, block, kind] = value.reshape(32, 8, 128).astype(BF)


def place_kernel(leaf_map, mid_map, pieces, out, total):
    column = column_at()
    total[...] = jnp.zeros_like(total)
    for front in range(4):
        pair = front // 2
        slot = mid_map[pair, leaf_map[front, column]] // 16
        for block in range(16):
            target = mid_map[pair, leaf_map[front, block]]
            piece = pieces[8 * front + block // 2, block % 2, 0]
            total[4 * target + slot] += piece.astype(F32)
    for pair in range(2):
        slots = [mid_map[pair, 16 * at + column] // 16 for at in range(2)]
        for block in range(32):
            target = mid_map[pair, block]
            for at in range(2):
                piece = pieces[16 * pair + block // 2, block % 2, 1 + at]
                total[4 * target + slots[at]] += piece.astype(F32)
    out[...] = total[...].reshape(64, 4, 8, 128).astype(BF)


def root_kernel(
    fill, panels, joined, front, out, root_factor, weights, panel, factor, turned
):
    cube, row, column = cube_at(), row_at(), column_at()
    slot = pl.program_id(0)

    @pl.when(slot == 0)
    def _():
        for at in range(8):
            span = slice(128 * at, 128 * at + 128)
            panel[:, span] = panels[at, 0]
            for owner in range(16):
                weights[64 * owner : 64 * owner + 64, span] = joined[owner, at]
        for at in range(0, 1024, 256):
            part = dot_t(panel[...], weights[at : at + 256])
            factor[:, at : at + 256] = (part * fill[16 * cube + row].astype(F32)).astype(BF)
        turned[...] = jnp.dot(factor[...], weights[...], preferred_element_type=F32).astype(BF)
        root_factor[...] = factor[:, pl.ds(pl.multiple_of(128 * column, 128), 128)]

    for half in range(2):
        for at in range(8):
            owner = 2 * ((at + column) % 8) + half
            piece = joined[owner, pl.ds(8 + 2 * slot, 2)].reshape(128, 128)
            panel[128 * half : 128 * half + 128, 128 * at : 128 * at + 128] = piece
    product = dot_t(turned[...], panel[...]) * fill[16 * slot + column].astype(F32)
    out[...] = front[...] - product


def add_kernel(base, arrived, out):
    for side in range(2):
        added = arrived[:, side, 0].astype(F32).reshape(256, 128)
        span = slice(128 * side, 128 * side + 128)
        out[:, span] = base[:, span] + added


def swap(value, axis):
    return lax.ppermute(value, axis, [(0, 1), (1, 0)])


def transpose(low, high):
    pairs = [[], []]
    for r in range(8):
        for c in range(8):
            for half in range(2):
                pairs[half].append((8 * r + c, 8 * (2 * ((c + r) % 8) + half) + r))
    plane = ROW + COL
    return lax.ppermute(low, plane, pairs[0]), lax.ppermute(high, plane, pairs[1])


def exchange(value, axes):
    return lax.all_to_all(value, axes, 0, 0, tiled=True)


def local(
    leaf_front,
    leaf_panel,
    leaf_inverse,
    leaf_fill,
    mid_front,
    mid_panel,
    mid_inverse,
    mid_fill,
    root_front,
    root_panel,
    root_inverse,
    root_fill,
    leaf_map,
    mid_map,
):
    piece = shape((256, 128))
    two, three = shape((2, 128, 128)), shape((3, 128, 128))
    panel_all = shape((8, 3, 256, 128))

    weights, spread, low, high = call(
        inputs_kernel,
        (shape((8, 3, 64, 128)), panel_all, three, three),
        (leaf_inverse, mid_inverse, root_inverse, leaf_panel, mid_panel, root_panel),
        60,
    )
    low, high = transpose(low, high)
    weights = exchange(weights, COL)
    whole, root_weights, kept, cross, last = call(
        whole_kernel,
        (shape((2, 64, 1024)), shape((8, 64, 128)), three, two, shape((128, 128))),
        (weights, low, high),
    )
    whole, spread = lax.optimization_barrier((whole, spread))
    weights = lax.all_gather(whole, ROW, axis=0, tiled=False)
    partner = swap(cross, "half")
    across = swap(last, "pair")
    corner = lax.ppermute(last, CUBE, [(0, 3), (1, 2), (2, 1), (3, 0)])
    panels = exchange(spread, COL)
    sent, joined = call(
        columns_kernel,
        (shape((8, 3, 128, 128)), shape((16, 64, 128))),
        (kept, partner, across, corner, root_weights),
        after=(panels,),
    )
    sent, joined, panels = lax.optimization_barrier((sent, joined, panels))
    joined = lax.all_gather(joined, ROW, axis=0, tiled=False)
    other_panels = swap(panels, "core")
    half_front = shape((3, 256, 128), F32)
    give_front = call(fronts_kernel, half_front, (leaf_front, mid_front))
    other_front = swap(give_front, "core")
    blocks = exchange(sent, "z")
    turned, keep, give = call(
        factor_kernel,
        (shape((512, 1024)), piece, piece),
        (leaf_fill, mid_fill),
        44,
        scratch=(
            pltpu.VMEM((512, 1024), BF),
            pltpu.VMEM((512, 1024), BF),
            pltpu.VMEM((512, 1024), F32),
            pltpu.VMEM((16, 64, 1024), BF),
            pltpu.VMEM((8, 256, 128), BF),
            pltpu.VMEM((8, 256, 128), BF),
            pltpu.SemaphoreType.DMA((3,)),
        ),
        after=(weights, panels, other_panels, other_front),
        cost=(2**31, 2**22),
    )
    other_turned = swap(turned, "core")
    blocks, other_turned = lax.optimization_barrier((blocks, other_turned))
    updates = call(
        update_kernel,
        shape((32, 2, 3, 8, 128)),
        (leaf_fill, mid_fill, turned, other_turned, blocks, leaf_front, mid_front, other_front),
        44,
        scratch=(pltpu.VMEM((3, 128, 1024), BF),),
    )
    given = swap(give, "core")
    leaf_first = lax.axis_index("core") == 0
    leaf_factor = jnp.where(leaf_first, keep, given)
    mid_factor = jnp.where(leaf_first, given, keep)
    pieces = exchange(updates, CUBE + ("z",))
    placed = call(
        place_kernel,
        shape((64, 4, 8, 128)),
        (leaf_map, mid_map, pieces),
        scratch=(pltpu.VMEM((256, 8, 128), F32),),
    )
    arrived = exchange(placed, CUBE + ROW)
    spot = pl.BlockSpec((256, 256), lambda s: (0, s))
    limit = pltpu.CompilerParams(vmem_limit_bytes=24 * 1024 * 1024)
    base, root_factor = pl.pallas_call(
        root_kernel,
        grid=(4,),
        out_shape=(shape((256, 1024), F32), piece),
        in_specs=[
            SMEM,
            pl.BlockSpec((8, 1, 256, 128), lambda s: (0, 2, 0, 0)),
            pl.BlockSpec((16, 16, 64, 128), lambda s: (0, 0, 0, 0)),
            spot,
        ],
        out_specs=(spot, pl.BlockSpec((256, 128), lambda s: (0, 0))),
        scratch_shapes=[
            pltpu.VMEM((1024, 1024), BF),
            pltpu.VMEM((256, 1024), BF),
            pltpu.VMEM((256, 1024), BF),
            pltpu.VMEM((256, 1024), BF),
        ],
        compiler_params=limit,
        cost_estimate=pl.CostEstimate(flops=2**32, bytes_accessed=2**23, transcendentals=0),
    )(root_fill, panels, joined, root_front)
    root_update = pl.pallas_call(
        add_kernel,
        grid=(4,),
        out_shape=shape((256, 1024), F32),
        in_specs=[spot, pl.BlockSpec((32, 2, 1, 8, 128), lambda s: (0, 0, s, 0, 0))],
        out_specs=spot,
        compiler_params=limit,
    )(base, arrived.reshape(32, 2, 4, 8, 128))
    return leaf_factor, mid_factor, root_factor, root_update


def solution(mesh):
    fine = Mesh(
        mesh.devices.reshape(2, 2, 8, 2, 2, 4), ("pair", "half", "z", "core", "ylo", "x")
    )
    block = P(CUBE + ROW, COL)
    in_specs = (
        block,
        block,
        P(CUBE, ROW, COL),
        P(),
        block,
        block,
        P(None, ROW, COL),
        P(),
        block,
        block,
        P(ROW, COL),
        P(),
        P(),
        P(),
    )
    return jax.shard_map(
        local, mesh=fine, in_specs=in_specs, out_specs=(block,) * 4, check_vma=False
    )
```
